512 devices in a mesh: dp: 16 (over z, core), cent: 32 (over x, y).
Axes of the slice: x: 4, y: 8, z: 8, core: 2. Of those that a mesh axis runs over, the one named last changes fastest.
Arguments:
- tokens: bfloat16 [32768, 128], P('dp'), may hold values from -6 to 20
- centroids: bfloat16 [16384, 128], P('cent'), may hold values from -6 to 6
- diagonal_factors: float32 [128], replicated, may hold values from 0.5 to 2
Outputs:
- new_centroids: float32 [16384, 128], P('cent')
- masses: float32 [16384], P('cent')
The draws below stay inside these ranges and needn't reach their ends.
All inputs are finite; a program needn't handle non-finite values.
Results may differ from the reference program's by a relative error of at most 0.0076.
Values sent between devices are 32-bit elements; how exact they have to be, the bound alone decides.
No kernel may reach another device: no remote copies, remote signals or barrier semaphores. Data moves between devices by JAX's collectives and lax.ppermute only.
A program may use at most 64 MiB of HBM per device.

```python
import math
import jax
import jax.numpy as jnp
from jax import lax

D = 128
TOK_DEV = 2048
ITERS = 3
EMBEDDING_TOTAL = 32768
CENTS = 16384
N_DP = 16


def draw_tokens(key, part):
    key = jax.random.fold_in(key, 11)
    first, second, third = jax.random.split(key, 3)
    base = jnp.clip(jax.random.normal(first, (EMBEDDING_TOTAL, D), jnp.float32), -6.0, 6.0)
    block_count = EMBEDDING_TOTAL // TOK_DEV
    picked = jax.random.randint(second, (block_count,), 0, TOK_DEV)
    rows = jnp.arange(EMBEDDING_TOTAL, dtype=jnp.int32)
    distant = (rows % TOK_DEV == picked[rows // TOK_DEV]).astype(jnp.float32)
    strength = jax.random.uniform(third, (EMBEDDING_TOTAL,), jnp.float32, 8.0, 14.0)
    columns = (jnp.arange(D, dtype=jnp.int32) < D // 2).astype(jnp.float32)
    shifted = base + (distant * strength)[:, None] * columns[None, :]
    return shifted.astype(jnp.bfloat16)


def levels(rng, shape, shards, smallest, high):
    def one(dim, shards_of):
        steps = jax.random.uniform(jax.random.fold_in(jax.random.fold_in(rng, 6), dim), (shards_of,), jnp.float32, smallest / len(shards), high / len(shards))
        return jnp.repeat(jnp.exp(steps), shape[dim] // shards_of).reshape((-1,) + (1,) * (len(shape) - dim - 1))

    gain = one(*shards[0])
    for cut in shards[1:]:
        gain = gain * one(*cut)
    return gain


def scatter_about(own_key, extent, width, most, cuts=(), kind=jnp.bfloat16):
    values = jax.random.normal(own_key, extent, jnp.float32) * width
    if len(cuts) > 0:
        values = levels(own_key, extent, cuts, -0.22, 0.18) * values
    return jnp.clip(values, min=-most, max=most).astype(kind)


def setup_inputs(seed: int = 0) -> dict:
    keys = jax.random.split(jax.random.key(seed), 4)
    tokens = draw_tokens(jax.random.fold_in(keys[3], 71), 0)
    centroids = scatter_about(keys[1], (CENTS, D), 1.0, 6.0, ((0, 32),))
    diagonal_factors = jnp.clip(jnp.exp(jax.random.uniform(keys[2], (D,), jnp.float32, math.log(0.5), math.log(2.0))), 0.5, 2.0)
    return {"tokens": tokens, "centroids": centroids, "diagonal_factors": diagonal_factors}


entropic_smoothing_factor = 4.0


def prepare(centroids, diagonal_factors):
    cent_float = centroids.astype(jnp.float32)
    rescaled_penalty = (cent_float * diagonal_factors[None, :]).astype(jnp.bfloat16)
    cluster_center_length_power = jnp.sum(cent_float * cent_float * diagonal_factors[None, :], axis=1)
    return rescaled_penalty, cluster_center_length_power


def quadratic_separation(embedding_group, rescaled_penalty, cluster_center_length_power, diagonal_factors):
    tok_float = embedding_group.astype(jnp.float32)
    tok_norm = jnp.sum(tok_float * tok_float * diagonal_factors[None, :], axis=1)
    cross = lax.dot_general(embedding_group, rescaled_penalty, (((1,), (1,)), ((), ())), preferred_element_type=jnp.float32)
    return tok_norm[:, None] + cluster_center_length_power[None, :] - 2.0 * cross


def reference(tokens, centroids, diagonal_factors):
    rescaled_penalty, cluster_center_length_power = prepare(centroids, diagonal_factors)
    blocks = tokens.reshape(N_DP, TOK_DEV, D)
    source_mass_logarithm = -math.log(EMBEDDING_TOTAL)
    target_mass_logarithm = -math.log(CENTS)
    source_side_multiplier = jnp.zeros((N_DP, TOK_DEV), jnp.float32)
    target_side_multiplier = jnp.zeros((CENTS,), jnp.float32)
    for iteration in range(ITERS):
        def col_step(carry, item):
            run_max, run_total = carry
            embedding_group, source_range_window = item
            unnormalized_affinity = (source_range_window[:, None] - quadratic_separation(embedding_group, rescaled_penalty, cluster_center_length_power, diagonal_factors)) / entropic_smoothing_factor
            new_max = jnp.maximum(run_max, jnp.max(unnormalized_affinity, axis=0))
            total = run_total * jnp.exp(run_max - new_max) + jnp.sum(jnp.exp(unnormalized_affinity - new_max[None, :]), axis=0)
            return (new_max, total), None

        start = (jnp.full((CENTS,), -jnp.inf, jnp.float32), jnp.zeros((CENTS,), jnp.float32))
        (target_side_largest, target_side_accumulated), unused = lax.scan(col_step, start, (blocks, source_side_multiplier))
        target_side_multiplier = entropic_smoothing_factor * (target_mass_logarithm - (target_side_largest + jnp.log(target_side_accumulated)))

        def row_step(embedding_group):
            unnormalized_affinity = (target_side_multiplier[None, :] - quadratic_separation(embedding_group, rescaled_penalty, cluster_center_length_power, diagonal_factors)) / entropic_smoothing_factor
            top = jnp.max(unnormalized_affinity, axis=1)
            return top + jnp.log(jnp.sum(jnp.exp(unnormalized_affinity - top[:, None]), axis=1))

        source_side_softmaximum = lax.map(row_step, blocks)
        source_side_multiplier = entropic_smoothing_factor * (source_mass_logarithm - source_side_softmaximum)

    def final_step(carry, item):
        numer, mass = carry
        embedding_group, source_range_window = item
        entrywise_separation = quadratic_separation(embedding_group, rescaled_penalty, cluster_center_length_power, diagonal_factors)
        assignment_share = jnp.exp((source_range_window[:, None] + target_side_multiplier[None, :] - entrywise_separation) / entropic_smoothing_factor + math.log(EMBEDDING_TOTAL))
        mass = mass + jnp.sum(assignment_share, axis=0)
        numer = numer + lax.dot_general(assignment_share.astype(jnp.bfloat16), embedding_group, (((0,), (0,)), ((), ())), preferred_element_type=jnp.float32)
        return (numer, mass), None

    start = (jnp.zeros((CENTS, D), jnp.float32), jnp.zeros((CENTS,), jnp.float32))
    (numer, mass), unused = lax.scan(final_step, start, (blocks, source_side_multiplier))
    new_centroids = numer / mass[:, None]
    masses = mass * (CENTS / EMBEDDING_TOTAL)
    return new_centroids, masses
```

```python
import math

import jax
import jax.numpy as jnp
from jax import lax
from jax.sharding import PartitionSpec as P

LANES = 128


def spread(vector, axis):
    size = lax.axis_size(axis)
    tile = vector.reshape(1, -1, LANES)
    copies = jnp.broadcast_to(tile, (size,) + tile.shape[1:])
    return lax.all_to_all(copies, axis, 0, 0).reshape(size, -1)


def spread_lse(vector, axis):
    parts = spread(vector, axis)
    top = jnp.max(parts, axis=0)
    return top + jnp.log(jnp.sum(jnp.exp(parts - top[None, :]), axis=0))


def spread_sum(vector, axis):
    return jnp.sum(spread(vector, axis), axis=0)


def shards(tokens, centroids, diagonal_factors):
    dp = lax.axis_size("dp")
    tok_local, dim = tokens.shape
    cent_local = centroids.shape[0]
    tok_count = tok_local * dp
    cent_count = cent_local * lax.axis_size("cent")
    ratio = tok_count / cent_count

    cent_float = centroids.astype(jnp.float32)
    scaled = (cent_float * diagonal_factors[None, :]).astype(jnp.bfloat16)
    cent_norm = jnp.sum(cent_float * cent_float * diagonal_factors[None, :], axis=1)
    tok_float = tokens.astype(jnp.float32)
    tok_norm = jnp.sum(tok_float * tok_float * diagonal_factors[None, :], axis=1)
    cross = lax.dot_general(
        scaled, tokens, (((1,), (1,)), ((), ())), preferred_element_type=jnp.float32
    )
    score = 0.5 * cross - 0.25 * tok_norm[None, :] - 0.25 * cent_norm[:, None]

    top = jnp.max(score, axis=1)
    part = top + jnp.log(jnp.sum(jnp.exp(score - top[:, None]), axis=1))
    col = -math.log(cent_count) - spread_lse(part, "dp")
    shifted = score + col[:, None]
    top = jnp.max(shifted, axis=0)
    kept = jnp.exp(shifted - top[None, :])
    part = top + jnp.log(jnp.sum(kept, axis=0))
    gain = jnp.exp(top - spread_lse(part, "cent"))

    weight = gain
    scale = None
    for iteration in range(2):
        mass = spread_sum(jnp.sum(kept * weight[None, :], axis=1), "dp")
        scale = ratio / mass
        rows = spread_sum(gain * jnp.sum(kept * scale[:, None], axis=0), "cent")
        weight = gain / rows

    share = kept * weight[None, :]
    mass_part = scale * jnp.sum(share, axis=1)
    numer_part = scale[:, None] * lax.dot_general(
        share.astype(jnp.bfloat16),
        tokens,
        (((1,), (0,)), ((), ())),
        preferred_element_type=jnp.float32,
    )
    rows = cent_local // dp
    packed = jnp.concatenate(
        [
            numer_part.reshape(dp, rows, dim),
            jnp.pad(mass_part.reshape(dp, 1, rows), ((0, 0), (0, 7), (0, dim - rows))),
        ],
        axis=1,
    )
    total = jnp.sum(lax.all_to_all(packed, "dp", 0, 0), axis=0)
    mass = total[rows, :rows]
    done = jnp.concatenate(
        [
            total[:rows] / mass[:, None],
            jnp.pad((mass / ratio)[None, :], ((0, 7), (0, dim - rows))),
        ],
        axis=0,
    )
    whole = lax.all_to_all(
        jnp.broadcast_to(done[None], (dp,) + done.shape), "dp", 0, 0
    )
    new_centroids = whole[:, :rows].reshape(cent_local, dim)
    masses = whole[:, rows, :rows].reshape(cent_local)
    return (new_centroids, masses)


def solution(mesh):
    return jax.shard_map(
        shards,
        mesh=mesh,
        in_specs=(P("dp", None), P("cent", None), P()),
        out_specs=(P("cent", None), P("cent")),
        check_vma=False,
    )
```

```python
import functools
import math

import jax
import jax.numpy as jnp
from jax import lax
from jax.experimental import pallas as pl
from jax.experimental.pallas import tpu as pltpu
from jax.sharding import PartitionSpec as P

LANES = 128
TILE = 256
F32 = jnp.float32
BF16 = jnp.bfloat16


def along_lanes(a, b):
    return lax.dot_general(a, b, (((1,), (1,)), ((), ())), preferred_element_type=F32)


def plain(a, b):
    return lax.dot_general(a, b, (((1,), (0,)), ((), ())), preferred_element_type=F32)


def combine_lse(parts_ref):
    parts = parts_ref[...]
    top = jnp.max(parts, axis=0)
    return top + jnp.log(jnp.sum(jnp.exp(parts - top[None]), axis=0))


def pair_of_rows(dense, k):
    return jnp.concatenate([dense[2 * k : 2 * k + 1], dense[2 * k + 1 : 2 * k + 2]], axis=1)


def two_terms(vector):
    wide = jnp.broadcast_to(vector, (16, vector.shape[1]))
    high = wide.astype(BF16)
    low = wide - high.astype(F32)
    row = lax.broadcasted_iota(jnp.int32, wide.shape, 0)
    return jnp.where(row == 0, high.astype(F32), jnp.where(row == 1, low, 0.0)).astype(BF16)


def dense_rows(vector):
    count = vector.shape[1] // LANES
    return jnp.concatenate(
        [vector[:, k * LANES : (k + 1) * LANES] for k in range(count)], axis=0
    )


def column_sums(kept_ref, weight):
    total = None
    for k in range(kept_ref.shape[1] // TILE):
        term = along_lanes(
            two_terms(pair_of_rows(weight, k)), kept_ref[:, k * TILE : (k + 1) * TILE]
        )
        total = term if total is None else total + term
    return dense_rows(jnp.sum(total, axis=0, keepdims=True))


def row_sums(kept_ref, scale):
    total = None
    for k in range(kept_ref.shape[0] // TILE):
        term = plain(two_terms(pair_of_rows(scale, k)), kept_ref[k * TILE : (k + 1) * TILE, :])
        total = term if total is None else total + term
    return dense_rows(jnp.sum(total, axis=0, keepdims=True))


def spread_out(out_ref, dense):
    out_ref[...] = jnp.broadcast_to(dense[None], out_ref.shape)


def first_columns(tok_ref, cent_ref, diag_ref, out_ref, half_ref):
    diag = diag_ref[...]
    half = (0.5 * (cent_ref[...].astype(F32) * diag).astype(BF16).astype(F32)).astype(BF16)
    half_ref[...] = half
    top = total = None
    for k in range(tok_ref.shape[0] // TILE):
        tok = tok_ref[k * TILE : (k + 1) * TILE, :]
        wide = tok.astype(F32)
        norm = 0.25 * jnp.sum(wide * wide * diag, axis=1, keepdims=True)
        score = along_lanes(tok, half) - norm
        here = jnp.max(score, axis=0, keepdims=True)
        new = here if top is None else jnp.maximum(top, here)
        part = jnp.sum(jnp.exp(score - new), axis=0, keepdims=True)
        total = part if top is None else total * jnp.exp(top - new) + part
        top = new
    spread_out(out_ref, dense_rows(top + jnp.log(total)))


def first_rows(cent_count, parts_ref, tok_ref, half_ref, norm_ref, kept_ref, top_ref, out_ref, sum_ref):
    norm = norm_ref[...]
    col = (-math.log(cent_count) - (combine_lse(parts_ref) - norm)) - norm
    column = jnp.concatenate(
        [jnp.broadcast_to(col[k : k + 1], (LANES, LANES)).T for k in range(col.shape[0])], axis=0
    )
    column = jnp.concatenate([column] * (TILE // LANES), axis=1)
    half = half_ref[...]
    for k in range(tok_ref.shape[0] // TILE):
        score = along_lanes(half, tok_ref[k * TILE : (k + 1) * TILE, :]) + column
        top = jnp.max(score, axis=0, keepdims=True)
        kept = jnp.exp(score - top)
        kept_ref[:, k * TILE : (k + 1) * TILE] = kept.astype(BF16)
        total = top + jnp.log(jnp.sum(kept, axis=0, keepdims=True))
        for h in range(TILE // LANES):
            at = k * (TILE // LANES) + h
            top_ref[at : at + 1, :] = top[:, h * LANES : (h + 1) * LANES]
            sum_ref[at : at + 1, :] = total[:, h * LANES : (h + 1) * LANES]
    spread_out(out_ref, sum_ref[...])


def second_columns(parts_ref, top_ref, norm_ref, kept_ref, out_ref, gain_ref):
    norm = norm_ref[...]
    gain = jnp.exp((top_ref[...] - norm) - (combine_lse(parts_ref) - norm))
    gain_ref[...] = gain
    spread_out(out_ref, column_sums(kept_ref, gain))


def later_rows(ratio, parts_ref, gain_ref, kept_ref, out_ref, scale_ref):
    scale = ratio / jnp.sum(parts_ref[...], axis=0)
    scale_ref[...] = scale
    spread_out(out_ref, gain_ref[...] * row_sums(kept_ref, scale))


def later_columns(parts_ref, gain_ref, kept_ref, out_ref):
    weight = gain_ref[...] / jnp.sum(parts_ref[...], axis=0)
    spread_out(out_ref, column_sums(kept_ref, weight))


def numerators(rows, parts_ref, gain_ref, kept_ref, tok_ref, out_ref):
    weight = gain_ref[...] / jnp.sum(parts_ref[...], axis=0)
    ones = jnp.ones((TILE, LANES), BF16)
    total = None
    for k in range(kept_ref.shape[1] // TILE):
        at = slice(k * TILE, (k + 1) * TILE)
        share = (kept_ref[:, at].astype(F32) * pair_of_rows(weight, k)).astype(BF16)
        term = plain(share, jnp.concatenate([tok_ref[at, :], ones], axis=1))
        total = term if total is None else total + term
    chunks = out_ref.shape[0]
    out_ref[:, :rows, :] = total[:, :LANES].reshape(chunks, rows, LANES)
    per = LANES // rows
    for g in range(total.shape[0] // LANES):
        mass = total[g * LANES : (g + 1) * LANES, LANES:].T[:8]
        for q in range(per):
            turned = mass if q == 0 else pltpu.roll(mass, LANES - q * rows, 1)
            out_ref[g * per + q, rows:, :] = turned


def divide(rows, parts_ref, out_ref):
    total = jnp.sum(parts_ref[...], axis=0)
    mass = jnp.broadcast_to(total[rows : rows + 1], (LANES, LANES)).T[:rows]
    out_ref[:, :rows, :] = jnp.broadcast_to(
        (total[:rows] / mass)[None], (out_ref.shape[0], rows, LANES)
    )
    out_ref[:, rows:, :] = jnp.broadcast_to(total[rows:][None], (out_ref.shape[0], 8, LANES))


def unpack(rows, ratio, parts_ref, scale_ref, cent_ref, mass_ref):
    cent_ref[...] = parts_ref[:, :rows, :].reshape(cent_ref.shape)
    per = LANES // rows
    lane = lax.broadcasted_iota(jnp.int32, (8, LANES), 1)
    for g in range(mass_ref.shape[0]):
        mass = parts_ref[g * per, rows:, :]
        for q in range(1, per):
            turned = pltpu.roll(parts_ref[g * per + q, rows:, :], q * rows, 1)
            mass = jnp.where(lane >= q * rows, turned, mass)
        mass_ref[g : g + 1, :] = mass[:1] * scale_ref[g : g + 1, :] / ratio


def run(kernel, outs, *operands, scratch=()):
    vmem = pl.BlockSpec(memory_space=pltpu.VMEM)
    return pl.pallas_call(
        kernel,
        out_shape=[jax.ShapeDtypeStruct(shape, kind) for shape, kind in outs],
        in_specs=[vmem] * len(operands),
        out_specs=[vmem] * len(outs),
        scratch_shapes=list(scratch),
        compiler_params=pltpu.CompilerParams(vmem_limit_bytes=24 * 1024 * 1024),
    )(*operands)


def shards(tokens, centroids, diagonal_factors):
    dp, cent = lax.axis_size("dp"), lax.axis_size("cent")
    tok_local, dim = tokens.shape
    cent_local = centroids.shape[0]
    cent_count = cent_local * cent
    ratio = tok_local * dp / cent_count
    rows = cent_local // dp
    by_tok, by_cent = (tok_local // LANES, LANES), (cent_local // LANES, LANES)
    to_dp, to_cent = (dp,) + by_cent, (cent,) + by_tok

    def quarter_norm(vectors):
        wide = vectors.astype(F32)
        return 0.25 * jnp.sum(wide * wide * diagonal_factors[None, :], axis=1)

    def over(axis, copies):
        return lax.all_to_all(copies, axis, 0, 0)

    tok_norm = quarter_norm(tokens).reshape(by_tok)
    cent_norm = quarter_norm(centroids).reshape(by_cent)

    copies, half = run(
        first_columns,
        [(to_dp, F32), ((cent_local, dim), BF16)],
        tokens,
        centroids,
        diagonal_factors.reshape(1, dim),
    )
    kept, top, copies = run(
        functools.partial(first_rows, cent_count),
        [((cent_local, tok_local), BF16), (by_tok, F32), (to_cent, F32)],
        over("dp", copies),
        tokens,
        half,
        cent_norm,
        scratch=[pltpu.VMEM(by_tok, F32)],
    )
    copies, gain = run(
        second_columns,
        [(to_dp, F32), (by_tok, F32)],
        over("cent", copies),
        top,
        tok_norm,
        kept,
    )
    rows_of = functools.partial(later_rows, ratio)
    rows_outs = [(to_cent, F32), (by_cent, F32)]
    copies, scale = run(rows_of, rows_outs, over("dp", copies), gain, kept)
    (copies,) = run(later_columns, [(to_dp, F32)], over("cent", copies), gain, kept)
    copies, scale = run(rows_of, rows_outs, over("dp", copies), gain, kept)

    packed = (dp, rows + 8, LANES)
    (copies,) = run(
        functools.partial(numerators, rows),
        [(packed, F32)],
        over("cent", copies),
        gain,
        kept,
        tokens,
    )
    (copies,) = run(functools.partial(divide, rows), [(packed, F32)], over("dp", copies))
    new_centroids, masses = run(
        functools.partial(unpack, rows, ratio),
        [((cent_local, dim), F32), (by_cent, F32)],
        over("dp", copies),
        scale,
    )
    return (new_centroids, masses.reshape(cent_local))


def solution(mesh):
    return jax.shard_map(
        shards,
        mesh=mesh,
        in_specs=(P("dp", None), P("cent", None), P()),
        out_specs=(P("cent", None), P("cent")),
        check_vma=False,
    )
```

```python
import functools
import math

import jax
import jax.numpy as jnp
from jax import lax
from jax.experimental import pallas as pl
from jax.experimental.pallas import tpu as pltpu
from jax.sharding import PartitionSpec as P

LANES = 128
TILE = 256
F32 = jnp.float32
BF16 = jnp.bfloat16


def along_lanes(a, b):
    return lax.dot_general(a, b, (((1,), (1,)), ((), ())), preferred_element_type=F32)


def plain(a, b):
    return lax.dot_general(a, b, (((1,), (0,)), ((), ())), preferred_element_type=F32)


def combine_lse(parts_ref):
    parts = parts_ref[...]
    top = jnp.max(parts, axis=0)
    return top + jnp.log(jnp.sum(jnp.exp(parts - top[None]), axis=0))


def pair_of_rows(dense, k):
    return jnp.concatenate([dense[2 * k : 2 * k + 1], dense[2 * k + 1 : 2 * k + 2]], axis=1)


def two_terms(vector):
    wide = jnp.broadcast_to(vector, (16, vector.shape[1]))
    high = wide.astype(BF16)
    low = wide - high.astype(F32)
    row = lax.broadcasted_iota(jnp.int32, wide.shape, 0)
    return jnp.where(row == 0, high.astype(F32), jnp.where(row == 1, low, 0.0)).astype(BF16)


def dense_rows(vector):
    count = vector.shape[1] // LANES
    return jnp.concatenate(
        [vector[:, k * LANES : (k + 1) * LANES] for k in range(count)], axis=0
    )


def column_sums(kept_ref, weight):
    total = None
    for k in range(kept_ref.shape[1] // TILE):
        term = along_lanes(
            two_terms(pair_of_rows(weight, k)), kept_ref[:, k * TILE : (k + 1) * TILE]
        )
        total = term if total is None else total + term
    return dense_rows(jnp.sum(total, axis=0, keepdims=True))


def row_sums(kept_ref, scale):
    total = None
    for k in range(kept_ref.shape[0] // TILE):
        term = plain(two_terms(pair_of_rows(scale, k)), kept_ref[k * TILE : (k + 1) * TILE, :])
        total = term if total is None else total + term
    return dense_rows(jnp.sum(total, axis=0, keepdims=True))


def spread_out(out_ref, dense):
    out_ref[...] = jnp.broadcast_to(dense[None], out_ref.shape)


def first_columns(tok_hbm, cent_hbm, diag_hbm, out_ref, half_ref, tok_ref, cent_ref, diag_ref, sems):
    loads = [
        pltpu.make_async_copy(cent_hbm, cent_ref, sems.at[0]),
        pltpu.make_async_copy(diag_hbm, diag_ref, sems.at[1]),
    ]
    tiles = []
    for k in range(tok_ref.shape[0] // TILE):
        at = pl.ds(k * TILE, TILE)
        tiles.append(pltpu.make_async_copy(tok_hbm.at[at], tok_ref.at[at], sems.at[2 + k]))
    for load in loads + tiles:
        load.start()
    for load in loads:
        load.wait()
    diag = diag_ref[...]
    half = (0.5 * (cent_ref[...].astype(F32) * diag).astype(BF16).astype(F32)).astype(BF16)
    half_ref[...] = half
    top = total = None
    for k, load in enumerate(tiles):
        load.wait()
        tok = tok_ref[k * TILE : (k + 1) * TILE, :]
        wide = tok.astype(F32)
        norm = 0.25 * jnp.sum(wide * wide * diag, axis=1, keepdims=True)
        score = along_lanes(tok, half) - norm
        here = jnp.max(score, axis=0, keepdims=True)
        new = here if top is None else jnp.maximum(top, here)
        part = jnp.sum(jnp.exp(score - new), axis=0, keepdims=True)
        total = part if top is None else total * jnp.exp(top - new) + part
        top = new
    spread_out(out_ref, dense_rows(top + jnp.log(total)))


def dense_norms(vectors_ref, diag, out_ref):
    for k in range(out_ref.shape[0]):
        wide = vectors_ref[k * LANES : (k + 1) * LANES, :].astype(F32)
        norm = 0.25 * jnp.sum(wide * wide * diag, axis=1, keepdims=True)
        out_ref[k : k + 1, :] = jnp.broadcast_to(norm, (LANES, LANES)).T[:1]


def prepare(tok_ref, cent_ref, diag_ref, half_ref, near_ref, near_half_ref, tok_norm_ref, cent_norm_ref):
    near_ref[...] = tok_ref[...]
    near_half_ref[...] = half_ref[...]
    dense_norms(tok_ref, diag_ref[...], tok_norm_ref)
    dense_norms(cent_ref, diag_ref[...], cent_norm_ref)


def first_rows(
    cent_count, parts_ref, tok_ref, half_ref, norm_ref, tok_norm_ref, kept_ref, top_ref, out_ref, sum_ref
):
    norm = norm_ref[...]
    col = (-math.log(cent_count) - (combine_lse(parts_ref) - norm)) - norm
    column = jnp.concatenate(
        [jnp.broadcast_to(col[k : k + 1], (LANES, LANES)).T for k in range(col.shape[0])], axis=0
    )
    column = jnp.concatenate([column] * (TILE // LANES), axis=1)
    half = half_ref[...]
    for k in range(tok_ref.shape[0] // TILE):
        score = along_lanes(half, tok_ref[k * TILE : (k + 1) * TILE, :]) + column
        top = jnp.max(score, axis=0, keepdims=True)
        kept = jnp.exp(score - top)
        kept_ref[:, k * TILE : (k + 1) * TILE] = kept.astype(BF16)
        total = top + jnp.log(jnp.sum(kept, axis=0, keepdims=True))
        for h in range(TILE // LANES):
            at = k * (TILE // LANES) + h
            top_ref[at : at + 1, :] = top[:, h * LANES : (h + 1) * LANES]
            sum_ref[at : at + 1, :] = total[:, h * LANES : (h + 1) * LANES]
    top_ref[...] = top_ref[...] - tok_norm_ref[...]
    spread_out(out_ref, sum_ref[...] - tok_norm_ref[...])


def second_columns(parts_ref, top_ref, kept_ref, out_ref, gain_ref):
    gain = jnp.exp(top_ref[...] - combine_lse(parts_ref))
    gain_ref[...] = gain
    spread_out(out_ref, column_sums(kept_ref, gain))


def later_rows(ratio, parts_ref, gain_ref, kept_ref, out_ref, scale_ref):
    scale = ratio / jnp.sum(parts_ref[...], axis=0)
    scale_ref[...] = scale
    spread_out(out_ref, gain_ref[...] * row_sums(kept_ref, scale))


def later_columns(parts_ref, gain_ref, kept_ref, out_ref):
    weight = gain_ref[...] / jnp.sum(parts_ref[...], axis=0)
    spread_out(out_ref, column_sums(kept_ref, weight))


def numerators(rows, parts_ref, gain_ref, kept_ref, tok_ref, out_ref):
    weight = gain_ref[...] / jnp.sum(parts_ref[...], axis=0)
    ones = jnp.ones((TILE, LANES), BF16)
    total = None
    for k in range(kept_ref.shape[1] // TILE):
        at = slice(k * TILE, (k + 1) * TILE)
        share = (kept_ref[:, at].astype(F32) * pair_of_rows(weight, k)).astype(BF16)
        term = plain(share, jnp.concatenate([tok_ref[at, :], ones], axis=1))
        total = term if total is None else total + term
    chunks = out_ref.shape[0]
    out_ref[:, :rows, :] = total[:, :LANES].reshape(chunks, rows, LANES)
    groups, per = total.shape[0] // LANES, LANES // rows
    mass = [total[g * LANES : (g + 1) * LANES, LANES:].T[:1] for g in range(groups)]
    for k in range(chunks):
        own = jnp.broadcast_to(mass[k // per], (8, LANES))
        if k % per:
            own = pltpu.roll(own, LANES - (k % per) * rows, 1)
        out_ref[k, rows:, :] = jnp.concatenate(mass + [own[: 8 - groups]], axis=0)


def divide(rows, ratio, parts_ref, scale_ref, out_ref, mass_ref):
    total = jnp.sum(parts_ref[...], axis=0)
    groups = mass_ref.shape[0]
    mass_ref[...] = total[rows : rows + groups] * scale_ref[...] / ratio
    own = total[rows + groups : rows + groups + 1]
    own = jnp.broadcast_to(own, (LANES, LANES)).T[:rows]
    spread_out(out_ref, total[:rows] / own)


def run(kernel, outs, *operands, scratch=(), place=pltpu.VMEM, room=24, cost=0):
    return pl.pallas_call(
        kernel,
        out_shape=[jax.ShapeDtypeStruct(shape, kind) for shape, kind in outs],
        in_specs=[pl.BlockSpec(memory_space=place)] * len(operands),
        out_specs=[pl.BlockSpec(memory_space=pltpu.VMEM)] * len(outs),
        scratch_shapes=list(scratch),
        cost_estimate=pl.CostEstimate(flops=cost, bytes_accessed=cost, transcendentals=0)
        if cost
        else None,
        compiler_params=pltpu.CompilerParams(vmem_limit_bytes=room * 1024 * 1024),
    )(*operands)


def shards(tokens, centroids, diagonal_factors):
    dp, cent = lax.axis_size("dp"), lax.axis_size("cent")
    tok_local, dim = tokens.shape
    cent_local = centroids.shape[0]
    cent_count = cent_local * cent
    ratio = tok_local * dp / cent_count
    rows = cent_local // dp
    by_tok, by_cent = (tok_local // LANES, LANES), (cent_local // LANES, LANES)
    to_dp, to_cent = (dp,) + by_cent, (cent,) + by_tok

    def over(axis, copies):
        return lax.all_to_all(copies, axis, 0, 0)

    diag = diagonal_factors.reshape(1, dim)
    copies, half = run(
        first_columns,
        [(to_dp, F32), ((cent_local, dim), BF16)],
        tokens,
        centroids,
        diag,
        scratch=[
            pltpu.VMEM((tok_local, dim), BF16),
            pltpu.VMEM((cent_local, dim), BF16),
            pltpu.VMEM((1, dim), F32),
            pltpu.SemaphoreType.DMA((2 + tok_local // TILE,)),
        ],
        place=pltpu.HBM,
        room=60,
    )
    near, near_half, tok_norm, cent_norm = run(
        prepare,
        [((tok_local, dim), BF16), ((cent_local, dim), BF16), (by_tok, F32), (by_cent, F32)],
        tokens,
        centroids,
        diag,
        half,
        cost=4 * (tok_local + cent_local) * dim,
    )
    kept, top, copies = run(
        functools.partial(first_rows, cent_count),
        [((cent_local, tok_local), BF16), (by_tok, F32), (to_cent, F32)],
        over("dp", copies),
        near,
        near_half,
        cent_norm,
        tok_norm,
        scratch=[pltpu.VMEM(by_tok, F32)],
    )
    copies, gain = run(
        second_columns,
        [(to_dp, F32), (by_tok, F32)],
        over("cent", copies),
        top,
        kept,
    )
    rows_of = functools.partial(later_rows, ratio)
    rows_outs = [(to_cent, F32), (by_cent, F32)]
    copies, scale = run(rows_of, rows_outs, over("dp", copies), gain, kept)
    (copies,) = run(later_columns, [(to_dp, F32)], over("cent", copies), gain, kept)
    copies, scale = run(rows_of, rows_outs, over("dp", copies), gain, kept)

    packed = (dp, rows + 8, LANES)
    (copies,) = run(
        functools.partial(numerators, rows),
        [(packed, F32)],
        over("cent", copies),
        gain,
        kept,
        near,
    )
    copies, masses = run(
        functools.partial(divide, rows, ratio),
        [((dp, rows, dim), F32), (by_cent, F32)],
        over("dp", copies),
        scale,
    )
    new_centroids = over("dp", copies).reshape(cent_local, dim)
    return (new_centroids, masses.reshape(cent_local))


def solution(mesh):
    return jax.shard_map(
        shards,
        mesh=mesh,
        in_specs=(P("dp", None), P("cent", None), P()),
        out_specs=(P("cent", None), P("cent")),
        check_vma=False,
    )
```

```python
import functools
import math

import jax
import jax.numpy as jnp
from jax import lax
from jax.experimental import pallas as pl
from jax.experimental.pallas import tpu as pltpu
from jax.sharding import PartitionSpec as P

LANES = 128
TILE = 256
F32 = jnp.float32
BF16 = jnp.bfloat16


def along_lanes(a, b):
    return lax.dot_general(a, b, (((1,), (1,)), ((), ())), preferred_element_type=F32)


def plain(a, b):
    return lax.dot_general(a, b, (((1,), (0,)), ((), ())), preferred_element_type=F32)


def combine_lse(parts_ref):
    parts = parts_ref[...]
    top = jnp.max(parts, axis=0)
    return top + jnp.log(jnp.sum(jnp.exp(parts - top[None]), axis=0))


def pair_of_rows(dense, k):
    return jnp.concatenate([dense[2 * k : 2 * k + 1], dense[2 * k + 1 : 2 * k + 2]], axis=1)


def two_terms(vector):
    wide = jnp.broadcast_to(vector, (16, vector.shape[1]))
    high = wide.astype(BF16)
    low = wide - high.astype(F32)
    row = lax.broadcasted_iota(jnp.int32, wide.shape, 0)
    return jnp.where(row == 0, high.astype(F32), jnp.where(row == 1, low, 0.0)).astype(BF16)


def dense_rows(vector):
    count = vector.shape[1] // LANES
    return jnp.concatenate(
        [vector[:, k * LANES : (k + 1) * LANES] for k in range(count)], axis=0
    )


def column_sums(kept_ref, weight):
    total = None
    for k in range(kept_ref.shape[1] // TILE):
        term = along_lanes(
            two_terms(pair_of_rows(weight, k)), kept_ref[:, k * TILE : (k + 1) * TILE]
        )
        total = term if total is None else total + term
    return dense_rows(jnp.sum(total, axis=0, keepdims=True))


def row_sums(kept_ref, scale):
    total = None
    for k in range(kept_ref.shape[0] // TILE):
        term = plain(two_terms(pair_of_rows(scale, k)), kept_ref[k * TILE : (k + 1) * TILE, :])
        total = term if total is None else total + term
    return dense_rows(jnp.sum(total, axis=0, keepdims=True))


def spread_out(out_ref, dense):
    out_ref[...] = jnp.broadcast_to(dense[None], out_ref.shape)


def half_scaled(cent_ref, diag):
    scaled = (cent_ref[...].astype(F32) * diag).astype(BF16)
    return (0.5 * scaled.astype(F32)).astype(BF16)


def first_columns(tok_hbm, cent_hbm, diag_hbm, out_ref, began_ref, tok_ref, cent_ref, diag_ref, sems):
    loads = [
        pltpu.make_async_copy(cent_hbm, cent_ref, sems.at[0]),
        pltpu.make_async_copy(diag_hbm, diag_ref, sems.at[1]),
        pltpu.make_async_copy(tok_hbm, tok_ref, sems.at[2]),
    ]
    for load in loads:
        load.start()
    for load in loads:
        load.wait()
    diag = diag_ref[...]
    half = half_scaled(cent_ref, diag)
    top = total = None
    for k in range(tok_ref.shape[0] // TILE):
        tok = tok_ref[k * TILE : (k + 1) * TILE, :]
        wide = tok.astype(F32)
        norm = 0.25 * jnp.sum(wide * wide * diag, axis=1, keepdims=True)
        score = along_lanes(tok, half) - norm
        here = jnp.max(score, axis=0, keepdims=True)
        new = here if top is None else jnp.maximum(top, here)
        part = jnp.sum(jnp.exp(score - new), axis=0, keepdims=True)
        total = part if top is None else total * jnp.exp(top - new) + part
        top = new
    spread_out(out_ref, dense_rows(top + jnp.log(total)))
    began_ref[...] = jnp.zeros_like(began_ref)


def dense_norms(vectors_ref, diag, out_ref):
    for k in range(out_ref.shape[0]):
        wide = vectors_ref[k * LANES : (k + 1) * LANES, :].astype(F32)
        norm = 0.25 * jnp.sum(wide * wide * diag, axis=1, keepdims=True)
        out_ref[k : k + 1, :] = jnp.broadcast_to(norm, (LANES, LANES)).T[:1]


def prepare(tok_ref, cent_ref, diag_ref, after_ref, near_ref, half_ref, tok_norm_ref, cent_norm_ref):
    del after_ref
    diag = diag_ref[...]
    near_ref[...] = tok_ref[...]
    half_ref[...] = half_scaled(cent_ref, diag)
    dense_norms(tok_ref, diag, tok_norm_ref)
    dense_norms(cent_ref, diag, cent_norm_ref)


def first_rows(
    cent_count, parts_ref, tok_ref, half_ref, norm_ref, tok_norm_ref, kept_ref, top_ref, out_ref, sum_ref
):
    norm = norm_ref[...]
    col = (-math.log(cent_count) - (combine_lse(parts_ref) - norm)) - norm
    column = jnp.concatenate(
        [jnp.broadcast_to(col[k : k + 1], (LANES, LANES)).T for k in range(col.shape[0])], axis=0
    )
    column = jnp.concatenate([column] * (TILE // LANES), axis=1)
    half = half_ref[...]
    for k in range(tok_ref.shape[0] // TILE):
        score = along_lanes(half, tok_ref[k * TILE : (k + 1) * TILE, :]) + column
        top = jnp.max(score, axis=0, keepdims=True)
        kept = jnp.exp(score - top)
        kept_ref[:, k * TILE : (k + 1) * TILE] = kept.astype(BF16)
        total = top + jnp.log(jnp.sum(kept, axis=0, keepdims=True))
        for h in range(TILE // LANES):
            at = k * (TILE // LANES) + h
            top_ref[at : at + 1, :] = top[:, h * LANES : (h + 1) * LANES]
            sum_ref[at : at + 1, :] = total[:, h * LANES : (h + 1) * LANES]
    top_ref[...] = top_ref[...] - tok_norm_ref[...]
    spread_out(out_ref, sum_ref[...] - tok_norm_ref[...])


def second_columns(parts_ref, top_ref, kept_ref, out_ref, gain_ref):
    gain = jnp.exp(top_ref[...] - combine_lse(parts_ref))
    gain_ref[...] = gain
    spread_out(out_ref, column_sums(kept_ref, gain))


def later_rows(ratio, parts_ref, gain_ref, kept_ref, out_ref, *scale_ref):
    scale = ratio / jnp.sum(parts_ref[...], axis=0)
    if scale_ref:
        scale_ref[0][...] = scale
    spread_out(out_ref, gain_ref[...] * row_sums(kept_ref, scale))


def later_columns(parts_ref, gain_ref, kept_ref, out_ref):
    weight = gain_ref[...] / jnp.sum(parts_ref[...], axis=0)
    spread_out(out_ref, column_sums(kept_ref, weight))


def numerators(rows, parts_ref, gain_ref, kept_ref, tok_ref, out_ref):
    weight = gain_ref[...] / jnp.sum(parts_ref[...], axis=0)
    ones = jnp.ones((TILE, LANES), BF16)
    total = None
    for k in range(kept_ref.shape[1] // TILE):
        at = slice(k * TILE, (k + 1) * TILE)
        share = (kept_ref[:, at].astype(F32) * pair_of_rows(weight, k)).astype(BF16)
        term = plain(share, jnp.concatenate([tok_ref[at, :], ones], axis=1))
        total = term if total is None else total + term
    chunks = out_ref.shape[0]
    out_ref[:, :rows, :] = total[:, :LANES].reshape(chunks, rows, LANES)
    groups, per = total.shape[0] // LANES, LANES // rows
    mass = [total[g * LANES : (g + 1) * LANES, LANES:].T[:1] for g in range(groups)]
    for k in range(chunks):
        own = jnp.broadcast_to(mass[k // per], (8, LANES))
        if k % per:
            own = pltpu.roll(own, LANES - (k % per) * rows, 1)
        out_ref[k, rows:, :] = jnp.concatenate(mass + [own[: 8 - groups]], axis=0)


def divide(rows, ratio, parts_ref, scale_ref, out_ref, mass_ref):
    total = jnp.sum(parts_ref[...], axis=0)
    groups = mass_ref.shape[0]
    mass_ref[...] = total[rows : rows + groups] * scale_ref[...] / ratio
    own = total[rows + groups : rows + groups + 1]
    own = jnp.broadcast_to(own, (LANES, LANES)).T[:rows]
    spread_out(out_ref, total[:rows] / own)


def finish(cent_ref, mass_ref, cent_hbm, mass_hbm, sems):
    stores = [
        pltpu.make_async_copy(cent_ref, cent_hbm, sems.at[0]),
        pltpu.make_async_copy(mass_ref, mass_hbm, sems.at[1]),
    ]
    for store in stores:
        store.start()
    for store in stores:
        store.wait()


def run(
    kernel,
    outs,
    *operands,
    scratch=(),
    place=pltpu.VMEM,
    out_place=pltpu.VMEM,
    room=24,
    cost=0,
):
    return pl.pallas_call(
        kernel,
        out_shape=[jax.ShapeDtypeStruct(shape, kind) for shape, kind in outs],
        in_specs=[pl.BlockSpec(memory_space=place)] * len(operands),
        out_specs=[pl.BlockSpec(memory_space=out_place)] * len(outs),
        scratch_shapes=list(scratch),
        cost_estimate=pl.CostEstimate(flops=cost, bytes_accessed=cost, transcendentals=0)
        if cost
        else None,
        compiler_params=pltpu.CompilerParams(vmem_limit_bytes=room * 1024 * 1024),
    )(*operands)


def shards(tokens, centroids, diagonal_factors):
    dp, cent = lax.axis_size("dp"), lax.axis_size("cent")
    tok_local, dim = tokens.shape
    cent_local = centroids.shape[0]
    cent_count = cent_local * cent
    ratio = tok_local * dp / cent_count
    rows = cent_local // dp
    by_tok, by_cent = (tok_local // LANES, LANES), (cent_local // LANES, LANES)
    to_dp, to_cent = (dp,) + by_cent, (cent,) + by_tok

    def over(axis, copies):
        return lax.all_to_all(copies, axis, 0, 0)

    diag = diagonal_factors.reshape(1, dim)
    copies, began = run(
        first_columns,
        [(to_dp, F32), ((8, LANES), F32)],
        tokens,
        centroids,
        diag,
        scratch=[
            pltpu.VMEM((tok_local, dim), BF16),
            pltpu.VMEM((cent_local, dim), BF16),
            pltpu.VMEM((1, dim), F32),
            pltpu.SemaphoreType.DMA((3,)),
        ],
        place=pltpu.HBM,
        room=60,
    )
    near, half, tok_norm, cent_norm = run(
        prepare,
        [((tok_local, dim), BF16), ((cent_local, dim), BF16), (by_tok, F32), (by_cent, F32)],
        tokens,
        centroids,
        diag,
        began,
        cost=4 * (tok_local + cent_local) * dim,
    )
    kept, top, copies = run(
        functools.partial(first_rows, cent_count),
        [((cent_local, tok_local), BF16), (by_tok, F32), (to_cent, F32)],
        over("dp", copies),
        near,
        half,
        cent_norm,
        tok_norm,
        scratch=[pltpu.VMEM(by_tok, F32)],
    )
    copies, gain = run(
        second_columns,
        [(to_dp, F32), (by_tok, F32)],
        over("cent", copies),
        top,
        kept,
    )
    rows_of = functools.partial(later_rows, ratio)
    rows_outs = [(to_cent, F32), (by_cent, F32)]
    (copies,) = run(rows_of, rows_outs[:1], over("dp", copies), gain, kept)
    (copies,) = run(later_columns, [(to_dp, F32)], over("cent", copies), gain, kept)
    copies, scale = run(rows_of, rows_outs, over("dp", copies), gain, kept)

    packed = (dp, rows + 8, LANES)
    (copies,) = run(
        functools.partial(numerators, rows),
        [(packed, F32)],
        over("cent", copies),
        gain,
        kept,
        near,
    )
    copies, masses = run(
        functools.partial(divide, rows, ratio),
        [((dp, rows, dim), F32), (by_cent, F32)],
        over("dp", copies),
        scale,
    )
    new_centroids, masses = run(
        finish,
        [((cent_local, dim), F32), (by_cent, F32)],
        over("dp", copies).reshape(cent_local, dim),
        masses,
        scratch=[pltpu.SemaphoreType.DMA((2,))],
        out_place=pltpu.HBM,
    )
    return (new_centroids, masses.reshape(cent_local))


def solution(mesh):
    return jax.shard_map(
        shards,
        mesh=mesh,
        in_specs=(P("dp", None), P("cent", None), P()),
        out_specs=(P("cent", None), P("cent")),
        check_vma=False,
    )
```

```python
import functools
import math

import jax
import jax.numpy as jnp
from jax import lax
from jax.experimental import pallas as pl
from jax.experimental.pallas import tpu as pltpu
from jax.sharding import Mesh
from jax.sharding import PartitionSpec as P

LANES = 128
TILE = 256
DP = ("z", "core")
F32 = jnp.float32
BF16 = jnp.bfloat16


def along_lanes(a, b):
    return lax.dot_general(a, b, (((1,), (1,)), ((), ())), preferred_element_type=F32)


def plain(a, b):
    return lax.dot_general(a, b, (((1,), (0,)), ((), ())), preferred_element_type=F32)


def combine_lse(parts_ref):
    parts = parts_ref[...]
    top = jnp.max(parts, axis=0)
    return top + jnp.log(jnp.sum(jnp.exp(parts - top[None]), axis=0))


def pair_of_rows(dense, k):
    return jnp.concatenate([dense[2 * k : 2 * k + 1], dense[2 * k + 1 : 2 * k + 2]], axis=1)


def two_terms(vector):
    wide = jnp.broadcast_to(vector, (16, vector.shape[1]))
    high = wide.astype(BF16)
    low = wide - high.astype(F32)
    row = lax.broadcasted_iota(jnp.int32, wide.shape, 0)
    return jnp.where(row == 0, high.astype(F32), jnp.where(row == 1, low, 0.0)).astype(BF16)


def dense_rows(vector):
    count = vector.shape[1] // LANES
    return jnp.concatenate(
        [vector[:, k * LANES : (k + 1) * LANES] for k in range(count)], axis=0
    )


def column_sums(kept_ref, weight):
    total = None
    for k in range(kept_ref.shape[1] // TILE):
        term = along_lanes(
            two_terms(pair_of_rows(weight, k)), kept_ref[:, k * TILE : (k + 1) * TILE]
        )
        total = term if total is None else total + term
    return dense_rows(jnp.sum(total, axis=0, keepdims=True))


def row_sums(kept_ref, scale):
    total = None
    for k in range(kept_ref.shape[0] // TILE):
        term = plain(two_terms(pair_of_rows(scale, k)), kept_ref[k * TILE : (k + 1) * TILE, :])
        total = term if total is None else total + term
    return dense_rows(jnp.sum(total, axis=0, keepdims=True))


def spread_out(out_ref, dense):
    out_ref[...] = jnp.broadcast_to(dense[None], out_ref.shape)


def half_scaled(cent_ref, diag):
    scaled = (cent_ref[...].astype(F32) * diag).astype(BF16)
    return (0.5 * scaled.astype(F32)).astype(BF16)


def first_columns(tok_hbm, cent_hbm, diag_hbm, out_ref, began_ref, tok_ref, cent_ref, diag_ref, sems):
    loads = [
        pltpu.make_async_copy(cent_hbm, cent_ref, sems.at[0]),
        pltpu.make_async_copy(diag_hbm, diag_ref, sems.at[1]),
        pltpu.make_async_copy(tok_hbm, tok_ref, sems.at[2]),
    ]
    for load in loads:
        load.start()
    for load in loads:
        load.wait()
    diag = diag_ref[...]
    half = half_scaled(cent_ref, diag)
    top = total = None
    for k in range(tok_ref.shape[0] // TILE):
        tok = tok_ref[k * TILE : (k + 1) * TILE, :]
        wide = tok.astype(F32)
        norm = 0.25 * jnp.sum(wide * wide * diag, axis=1, keepdims=True)
        score = along_lanes(tok, half) - norm
        here = jnp.max(score, axis=0, keepdims=True)
        new = here if top is None else jnp.maximum(top, here)
        part = jnp.sum(jnp.exp(score - new), axis=0, keepdims=True)
        total = part if top is None else total * jnp.exp(top - new) + part
        top = new
    spread_out(out_ref, dense_rows(top + jnp.log(total)))
    began_ref[...] = jnp.zeros_like(began_ref)


def dense_norms(vectors_ref, diag, out_ref):
    for k in range(out_ref.shape[0]):
        wide = vectors_ref[k * LANES : (k + 1) * LANES, :].astype(F32)
        norm = 0.25 * jnp.sum(wide * wide * diag, axis=1, keepdims=True)
        out_ref[k : k + 1, :] = jnp.broadcast_to(norm, (LANES, LANES)).T[:1]


def prepare(tok_ref, cent_ref, diag_ref, after_ref, near_ref, half_ref, tok_norm_ref, cent_norm_ref):
    del after_ref
    diag = diag_ref[...]
    near_ref[...] = tok_ref[...]
    half_ref[...] = half_scaled(cent_ref, diag)
    dense_norms(tok_ref, diag, tok_norm_ref)
    dense_norms(cent_ref, diag, cent_norm_ref)


def first_rows(
    cent_count, parts_ref, tok_ref, half_ref, norm_ref, tok_norm_ref, kept_ref, top_ref, out_ref, sum_ref
):
    norm = norm_ref[...]
    col = (-math.log(cent_count) - (combine_lse(parts_ref) - norm)) - norm
    column = jnp.concatenate(
        [jnp.broadcast_to(col[k : k + 1], (LANES, LANES)).T for k in range(col.shape[0])], axis=0
    )
    column = jnp.concatenate([column] * (TILE // LANES), axis=1)
    half = half_ref[...]
    for k in range(tok_ref.shape[0] // TILE):
        score = along_lanes(half, tok_ref[k * TILE : (k + 1) * TILE, :]) + column
        top = jnp.max(score, axis=0, keepdims=True)
        kept = jnp.exp(score - top)
        kept_ref[:, k * TILE : (k + 1) * TILE] = kept.astype(BF16)
        total = top + jnp.log(jnp.sum(kept, axis=0, keepdims=True))
        for h in range(TILE // LANES):
            at = k * (TILE // LANES) + h
            top_ref[at : at + 1, :] = top[:, h * LANES : (h + 1) * LANES]
            sum_ref[at : at + 1, :] = total[:, h * LANES : (h + 1) * LANES]
    top_ref[...] = top_ref[...] - tok_norm_ref[...]
    spread_out(out_ref, sum_ref[...] - tok_norm_ref[...])


def second_columns(parts_ref, top_ref, kept_ref, out_ref, gain_ref):
    gain = jnp.exp(top_ref[...] - combine_lse(parts_ref))
    gain_ref[...] = gain
    spread_out(out_ref, column_sums(kept_ref, gain))


def later_rows(ratio, parts_ref, gain_ref, kept_ref, out_ref, *scale_ref):
    scale = ratio / jnp.sum(parts_ref[...], axis=0)
    if scale_ref:
        scale_ref[0][...] = scale
    spread_out(out_ref, gain_ref[...] * row_sums(kept_ref, scale))


def later_columns(parts_ref, gain_ref, kept_ref, out_ref):
    weight = gain_ref[...] / jnp.sum(parts_ref[...], axis=0)
    spread_out(out_ref, column_sums(kept_ref, weight))


def numerators(rows, parts_ref, gain_ref, kept_ref, tok_ref, out_ref):
    weight = gain_ref[...] / jnp.sum(parts_ref[...], axis=0)
    ones = jnp.ones((TILE, LANES), BF16)
    total = None
    for k in range(kept_ref.shape[1] // TILE):
        at = slice(k * TILE, (k + 1) * TILE)
        share = (kept_ref[:, at].astype(F32) * pair_of_rows(weight, k)).astype(BF16)
        term = plain(share, jnp.concatenate([tok_ref[at, :], ones], axis=1))
        total = term if total is None else total + term
    chunks = out_ref.shape[0]
    out_ref[:, :rows, :] = total[:, :LANES].reshape(chunks, rows, LANES)
    groups, per = total.shape[0] // LANES, LANES // rows
    mass = [total[g * LANES : (g + 1) * LANES, LANES:].T[:1] for g in range(groups)]
    for k in range(chunks):
        own = jnp.broadcast_to(mass[k // per], (8, LANES))
        if k % per:
            own = pltpu.roll(own, LANES - (k % per) * rows, 1)
        out_ref[k, rows:, :] = jnp.concatenate(mass + [own[: 8 - groups]], axis=0)


def divide(rows, ratio, parts_ref, scale_ref, out_ref, mass_ref):
    total = jnp.sum(parts_ref[...], axis=0)
    groups = mass_ref.shape[0]
    mass_ref[...] = total[rows : rows + groups] * scale_ref[...] / ratio
    own = total[rows + groups : rows + groups + 1]
    own = jnp.broadcast_to(own, (LANES, LANES)).T[:rows]
    spread_out(out_ref, total[:rows] / own)


def finish(cent_ref, mass_ref, cent_hbm, mass_hbm, sems):
    cores = cent_ref.shape[0]
    stores = [pltpu.make_async_copy(mass_ref, mass_hbm, sems.at[cores])]
    for c in range(cores):
        stores.append(pltpu.make_async_copy(cent_ref.at[c], cent_hbm.at[:, c], sems.at[c]))
    for store in stores:
        store.start()
    for store in stores:
        store.wait()


def run(
    kernel,
    outs,
    *operands,
    scratch=(),
    place=pltpu.VMEM,
    out_place=pltpu.VMEM,
    room=24,
    cost=0,
):
    return pl.pallas_call(
        kernel,
        out_shape=[jax.ShapeDtypeStruct(shape, kind) for shape, kind in outs],
        in_specs=[pl.BlockSpec(memory_space=place)] * len(operands),
        out_specs=[pl.BlockSpec(memory_space=out_place)] * len(outs),
        scratch_shapes=list(scratch),
        cost_estimate=pl.CostEstimate(flops=cost, bytes_accessed=cost, transcendentals=0)
        if cost
        else None,
        compiler_params=pltpu.CompilerParams(vmem_limit_bytes=room * 1024 * 1024),
    )(*operands)


def shards(tokens, centroids, diagonal_factors):
    chips, cores, cent = (lax.axis_size(axis) for axis in ("z", "core", "cent"))
    dp = chips * cores
    tok_local, dim = tokens.shape
    cent_local = centroids.shape[0]
    cent_count = cent_local * cent
    ratio = tok_local * dp / cent_count
    rows = cent_local // dp
    by_tok, by_cent = (tok_local // LANES, LANES), (cent_local // LANES, LANES)
    to_dp, to_cent = (dp,) + by_cent, (cent,) + by_tok

    def over(axis, copies):
        return lax.all_to_all(copies, axis, 0, 0)

    diag = diagonal_factors.reshape(1, dim)
    copies, began = run(
        first_columns,
        [(to_dp, F32), ((8, LANES), F32)],
        tokens,
        centroids,
        diag,
        scratch=[
            pltpu.VMEM((tok_local, dim), BF16),
            pltpu.VMEM((cent_local, dim), BF16),
            pltpu.VMEM((1, dim), F32),
            pltpu.SemaphoreType.DMA((3,)),
        ],
        place=pltpu.HBM,
        room=60,
    )
    near, half, tok_norm, cent_norm = run(
        prepare,
        [((tok_local, dim), BF16), ((cent_local, dim), BF16), (by_tok, F32), (by_cent, F32)],
        tokens,
        centroids,
        diag,
        began,
        cost=4 * (tok_local + cent_local) * dim,
    )
    kept, top, copies = run(
        functools.partial(first_rows, cent_count),
        [((cent_local, tok_local), BF16), (by_tok, F32), (to_cent, F32)],
        over(DP, copies),
        near,
        half,
        cent_norm,
        tok_norm,
        scratch=[pltpu.VMEM(by_tok, F32)],
    )
    copies, gain = run(
        second_columns,
        [(to_dp, F32), (by_tok, F32)],
        over("cent", copies),
        top,
        kept,
    )
    rows_of = functools.partial(later_rows, ratio)
    rows_outs = [(to_cent, F32), (by_cent, F32)]
    (copies,) = run(rows_of, rows_outs[:1], over(DP, copies), gain, kept)
    (copies,) = run(later_columns, [(to_dp, F32)], over("cent", copies), gain, kept)
    copies, scale = run(rows_of, rows_outs, over(DP, copies), gain, kept)

    packed = (dp, rows + 8, LANES)
    (copies,) = run(
        functools.partial(numerators, rows),
        [(packed, F32)],
        over("cent", copies),
        gain,
        kept,
        near,
    )
    copies, masses = run(
        functools.partial(divide, rows, ratio),
        [((chips, rows, dim), F32), (by_cent, F32)],
        over(DP, copies),
        scale,
    )
    halves = lax.all_gather(over("z", copies), "core")
    new_centroids, masses = run(
        finish,
        [((chips, cores, rows, dim), F32), (by_cent, F32)],
        halves,
        masses,
        scratch=[pltpu.SemaphoreType.DMA((cores + 1,))],
        out_place=pltpu.HBM,
    )
    return (new_centroids.reshape(cent_local, dim), masses.reshape(cent_local))


def solution(mesh):
    dp, cent = mesh.devices.shape
    split = Mesh(mesh.devices.reshape(dp // 2, 2, cent), DP + ("cent",))
    return jax.shard_map(
        shards,
        mesh=split,
        in_specs=(P(DP, None), P("cent", None), P()),
        out_specs=(P("cent", None), P("cent")),
        check_vma=False,
    )
```

```python
import functools
import math

import jax
import jax.numpy as jnp
from jax import lax
from jax.experimental import pallas as pl
from jax.experimental.pallas import tpu as pltpu
from jax.sharding import Mesh
from jax.sharding import PartitionSpec as P

LANES = 128
TILE = 256
DP = ("z", "core")
CENT = ("outer", "inner", "y")
F32 = jnp.float32
BF16 = jnp.bfloat16


def along_lanes(a, b):
    return lax.dot_general(a, b, (((1,), (1,)), ((), ())), preferred_element_type=F32)


def plain(a, b):
    return lax.dot_general(a, b, (((1,), (0,)), ((), ())), preferred_element_type=F32)


def combine_lse(parts_ref):
    parts = parts_ref[...]
    top = jnp.max(parts, axis=0)
    return top + jnp.log(jnp.sum(jnp.exp(parts - top[None]), axis=0))


def pair_of_rows(dense, k):
    return jnp.concatenate([dense[2 * k : 2 * k + 1], dense[2 * k + 1 : 2 * k + 2]], axis=1)


def two_terms(vector):
    wide = jnp.broadcast_to(vector, (16, vector.shape[1]))
    high = wide.astype(BF16)
    low = wide - high.astype(F32)
    row = lax.broadcasted_iota(jnp.int32, wide.shape, 0)
    return jnp.where(row == 0, high.astype(F32), jnp.where(row == 1, low, 0.0)).astype(BF16)


def dense_rows(vector):
    count = vector.shape[1] // LANES
    return jnp.concatenate(
        [vector[:, k * LANES : (k + 1) * LANES] for k in range(count)], axis=0
    )


def column_sums(kept_ref, weight):
    total = None
    for k in range(kept_ref.shape[1] // TILE):
        term = along_lanes(
            two_terms(pair_of_rows(weight, k)), kept_ref[:, k * TILE : (k + 1) * TILE]
        )
        total = term if total is None else total + term
    return dense_rows(jnp.sum(total, axis=0, keepdims=True))


def row_sums(kept_ref, scale):
    total = None
    for k in range(kept_ref.shape[0] // TILE):
        term = plain(two_terms(pair_of_rows(scale, k)), kept_ref[k * TILE : (k + 1) * TILE, :])
        total = term if total is None else total + term
    return dense_rows(jnp.sum(total, axis=0, keepdims=True))


def spread_out(out_ref, dense):
    out_ref[...] = jnp.broadcast_to(dense[None], out_ref.shape)


def half_scaled(cent_ref, diag):
    scaled = (cent_ref[...].astype(F32) * diag).astype(BF16)
    return (0.5 * scaled.astype(F32)).astype(BF16)


def first_columns(tok_hbm, cent_hbm, diag_hbm, out_ref, began_ref, tok_ref, cent_ref, diag_ref, sems):
    loads = [
        pltpu.make_async_copy(cent_hbm, cent_ref, sems.at[0]),
        pltpu.make_async_copy(diag_hbm, diag_ref, sems.at[1]),
        pltpu.make_async_copy(tok_hbm, tok_ref, sems.at[2]),
    ]
    for load in loads:
        load.start()
    for load in loads:
        load.wait()
    diag = diag_ref[...]
    half = half_scaled(cent_ref, diag)
    top = total = None
    for k in range(tok_ref.shape[0] // TILE):
        tok = tok_ref[k * TILE : (k + 1) * TILE, :]
        wide = tok.astype(F32)
        norm = 0.25 * jnp.sum(wide * wide * diag, axis=1, keepdims=True)
        score = along_lanes(tok, half) - norm
        here = jnp.max(score, axis=0, keepdims=True)
        new = here if top is None else jnp.maximum(top, here)
        part = jnp.sum(jnp.exp(score - new), axis=0, keepdims=True)
        total = part if top is None else total * jnp.exp(top - new) + part
        top = new
    spread_out(out_ref, dense_rows(top + jnp.log(total)))
    began_ref[...] = jnp.zeros_like(began_ref)


def dense_norms(vectors_ref, diag, out_ref):
    for k in range(out_ref.shape[0]):
        wide = vectors_ref[k * LANES : (k + 1) * LANES, :].astype(F32)
        norm = 0.25 * jnp.sum(wide * wide * diag, axis=1, keepdims=True)
        out_ref[k : k + 1, :] = jnp.broadcast_to(norm, (LANES, LANES)).T[:1]


def prepare(tok_ref, cent_ref, diag_ref, after_ref, near_ref, half_ref, tok_norm_ref, cent_norm_ref):
    del after_ref
    diag = diag_ref[...]
    near_ref[...] = tok_ref[...]
    half_ref[...] = half_scaled(cent_ref, diag)
    dense_norms(tok_ref, diag, tok_norm_ref)
    dense_norms(cent_ref, diag, cent_norm_ref)


def keep_rows(half, col, tok_ref, start, kept_ref, top_ref, sum_ref):
    column = jnp.concatenate(
        [jnp.broadcast_to(col[k : k + 1], (LANES, LANES)).T for k in range(col.shape[0])], axis=0
    )
    column = jnp.concatenate([column] * (TILE // LANES), axis=1)
    for k in range(kept_ref.shape[1] // TILE):
        tok = tok_ref[pl.ds(pl.multiple_of(start + k * TILE, TILE), TILE), :]
        score = along_lanes(half, tok) + column
        top = jnp.max(score, axis=0, keepdims=True)
        kept = jnp.exp(score - top)
        kept_ref[:, k * TILE : (k + 1) * TILE] = kept.astype(BF16)
        total = None
        if sum_ref is not None:
            total = top + jnp.log(jnp.sum(kept, axis=0, keepdims=True))
        for h in range(TILE // LANES):
            at = k * (TILE // LANES) + h
            top_ref[at : at + 1, :] = top[:, h * LANES : (h + 1) * LANES]
            if sum_ref is not None:
                sum_ref[at : at + 1, :] = total[:, h * LANES : (h + 1) * LANES]


def first_rows(
    cent_count,
    parts_ref,
    tok_ref,
    half_ref,
    norm_ref,
    tok_norm_ref,
    kept_ref,
    out_ref,
    give_ref,
    top_ref,
    sum_ref,
):
    norm = norm_ref[...]
    col = (-math.log(cent_count) - (combine_lse(parts_ref) - norm)) - norm
    half = half_ref[...]
    give_ref[: half.shape[0], :] = half.astype(F32)
    give_ref[half.shape[0] : half.shape[0] + 8, :] = jnp.concatenate([col, col], axis=0)[:8]
    keep_rows(half, col, tok_ref, 0, kept_ref, top_ref, sum_ref)
    give_ref[half.shape[0] + 8 :, :] = top_ref[...] - tok_norm_ref[...]
    spread_out(out_ref, sum_ref[...] - tok_norm_ref[...])


def neighbour_rows(give_ref, other_ref, half_ref, tok_ref, tok_norm_ref, kept_ref, tops_ref):
    place = lax.axis_index("inner")
    count = half_ref.shape[0]
    groups = count // LANES
    half = jnp.concatenate([half_ref[...], other_ref[:count, :].astype(BF16)], axis=0)
    col = jnp.concatenate(
        [give_ref[count : count + groups, :], other_ref[count : count + groups, :]], axis=0
    )
    own, share = tok_norm_ref.shape[0], tok_norm_ref.shape[0] // 2
    tops_ref[:own, :] = give_ref[give_ref.shape[0] - own :, :]
    top_ref = tops_ref.at[own:]
    keep_rows(half, col, tok_ref, place * kept_ref.shape[1], kept_ref, top_ref, None)
    norm = tok_norm_ref[pl.ds(pl.multiple_of(place * share, share), share), :]
    top_ref[...] = top_ref[...] - norm


def choose(place, first, second):
    return jnp.where(jnp.broadcast_to(place, first.shape) == 0, first, second)


def second_columns(parts_ref, tops_ref, kept_ref, out_ref, gain_ref, near_gain_ref):
    total = combine_lse(parts_ref)
    own, share = gain_ref.shape[0], near_gain_ref.shape[0]
    gain = jnp.exp(tops_ref[:own, :] - total)
    gain_ref[...] = gain
    mine = choose(lax.axis_index("inner"), total[:share], total[share:])
    near_gain_ref[...] = jnp.exp(tops_ref[own:, :] - mine)
    spread_out(out_ref, column_sums(kept_ref, gain))


def later_rows(ratio, parts_ref, gain_ref, kept_ref, out_ref, *scale_ref):
    place = lax.axis_index("inner")
    parts = parts_ref[...]
    both = jnp.sum(parts.reshape((parts.shape[0] // 2, 2) + parts.shape[1:]), axis=0)
    scale = ratio / choose(place, both[0], both[1])
    other = ratio / choose(place, both[1], both[0])
    if scale_ref:
        scale_ref[0][...] = scale
    scales = jnp.concatenate([scale, other], axis=0)
    spread_out(out_ref, gain_ref[...] * row_sums(kept_ref, scales))


def all_rows(outer, parts_ref):
    parts = parts_ref[...]
    parts = parts.reshape((outer, 2, parts.shape[0] // (2 * outer)) + parts.shape[1:])
    both = jnp.sum(jnp.sum(parts, axis=2), axis=0)
    return jnp.concatenate([both[0], both[1]], axis=0)


def later_columns(outer, parts_ref, gain_ref, kept_ref, out_ref):
    weight = gain_ref[...] / all_rows(outer, parts_ref)
    spread_out(out_ref, column_sums(kept_ref, weight))


def numerators(rows, outer, parts_ref, gain_ref, kept_ref, tok_ref, out_ref):
    weight = gain_ref[...] / all_rows(outer, parts_ref)
    ones = jnp.ones((TILE, LANES), BF16)
    total = None
    for k in range(kept_ref.shape[1] // TILE):
        at = slice(k * TILE, (k + 1) * TILE)
        share = (kept_ref[:, at].astype(F32) * pair_of_rows(weight, k)).astype(BF16)
        term = plain(share, jnp.concatenate([tok_ref[at, :], ones], axis=1))
        total = term if total is None else total + term
    chunks = out_ref.shape[0]
    out_ref[:, :rows, :] = total[:, :LANES].reshape(chunks, rows, LANES)
    groups, per = total.shape[0] // LANES, LANES // rows
    mass = [total[g * LANES : (g + 1) * LANES, LANES:].T[:1] for g in range(groups)]
    for k in range(chunks):
        own = jnp.broadcast_to(mass[k // per], (8, LANES))
        if k % per:
            own = pltpu.roll(own, LANES - (k % per) * rows, 1)
        out_ref[k, rows:, :] = jnp.concatenate(mass + [own[: 8 - groups]], axis=0)


def divide(rows, ratio, parts_ref, scale_ref, out_ref, mass_ref):
    total = jnp.sum(parts_ref[...], axis=0)
    groups = mass_ref.shape[0]
    mass_ref[...] = total[rows : rows + groups] * scale_ref[...] / ratio
    own = total[rows + groups : rows + groups + 1]
    own = jnp.broadcast_to(own, (LANES, LANES)).T[:rows]
    spread_out(out_ref, total[:rows] / own)


def finish(cent_ref, mass_ref, cent_hbm, mass_hbm, sems):
    cores = cent_ref.shape[0]
    stores = [pltpu.make_async_copy(mass_ref, mass_hbm, sems.at[cores])]
    for c in range(cores):
        stores.append(pltpu.make_async_copy(cent_ref.at[c], cent_hbm.at[:, c], sems.at[c]))
    for store in stores:
        store.start()
    for store in stores:
        store.wait()


def run(
    kernel,
    outs,
    *operands,
    scratch=(),
    place=pltpu.VMEM,
    out_place=pltpu.VMEM,
    room=24,
    cost=0,
):
    return pl.pallas_call(
        kernel,
        out_shape=[jax.ShapeDtypeStruct(shape, kind) for shape, kind in outs],
        in_specs=[pl.BlockSpec(memory_space=place)] * len(operands),
        out_specs=[pl.BlockSpec(memory_space=out_place)] * len(outs),
        scratch_shapes=list(scratch),
        cost_estimate=pl.CostEstimate(flops=cost, bytes_accessed=cost, transcendentals=0)
        if cost
        else None,
        compiler_params=pltpu.CompilerParams(vmem_limit_bytes=room * 1024 * 1024),
    )(*operands)


def shards(tokens, centroids, diagonal_factors):
    chips, cores, outer = (lax.axis_size(axis) for axis in ("z", "core", "outer"))
    dp, cent = chips * cores, lax.axis_size(CENT)
    tok_local, dim = tokens.shape
    cent_local = centroids.shape[0]
    cent_count = cent_local * cent
    ratio = tok_local * dp / cent_count
    rows = cent_local // dp
    by_tok, by_cent = (tok_local // LANES, LANES), (cent_local // LANES, LANES)
    to_dp, to_cent = (dp,) + by_cent, (cent,) + by_tok
    by_half = (by_tok[0] // 2, LANES)
    to_both, to_half = (2 * dp,) + by_cent, (cent,) + by_half

    def over(axis, copies):
        return lax.all_to_all(copies, axis, 0, 0)

    diag = diagonal_factors.reshape(1, dim)
    copies, began = run(
        first_columns,
        [(to_dp, F32), ((8, LANES), F32)],
        tokens,
        centroids,
        diag,
        scratch=[
            pltpu.VMEM((tok_local, dim), BF16),
            pltpu.VMEM((cent_local, dim), BF16),
            pltpu.VMEM((1, dim), F32),
            pltpu.SemaphoreType.DMA((3,)),
        ],
        place=pltpu.HBM,
        room=60,
    )
    near, half, tok_norm, cent_norm = run(
        prepare,
        [((tok_local, dim), BF16), ((cent_local, dim), BF16), (by_tok, F32), (by_cent, F32)],
        tokens,
        centroids,
        diag,
        began,
        cost=4 * (tok_local + cent_local) * dim,
    )
    kept, copies, give = run(
        functools.partial(first_rows, cent_count),
        [
            ((cent_local, tok_local), BF16),
            (to_cent, F32),
            ((cent_local + 8 + by_tok[0], dim), F32),
        ],
        over(DP, copies),
        near,
        half,
        cent_norm,
        tok_norm,
        scratch=[pltpu.VMEM(by_tok, F32)] * 2,
    )
    other = lax.ppermute(give, "inner", [(0, 1), (1, 0)])
    near_kept, tops = run(
        neighbour_rows,
        [((2 * cent_local, tok_local // 2), BF16), ((by_tok[0] + by_half[0], LANES), F32)],
        give,
        other,
        half,
        near,
        tok_norm,
        cost=cent_local * tok_local * 2 * dim,
    )
    copies, gain, near_gain = run(
        second_columns,
        [(to_both, F32), (by_tok, F32), (by_half, F32)],
        over(CENT, copies),
        tops,
        kept,
    )
    rows_of = functools.partial(later_rows, ratio)
    rows_outs = [(to_half, F32), (by_cent, F32)]
    both = DP + ("inner",)
    (copies,) = run(
        rows_of, rows_outs[:1], over(both, copies), near_gain, near_kept
    )
    (copies,) = run(
        functools.partial(later_columns, outer), [(to_both, F32)], over(CENT, copies), gain, kept
    )
    copies, scale = run(
        rows_of, rows_outs, over(both, copies), near_gain, near_kept
    )

    packed = (dp, rows + 8, LANES)
    (copies,) = run(
        functools.partial(numerators, rows, outer),
        [(packed, F32)],
        over(CENT, copies),
        gain,
        kept,
        near,
    )
    copies, masses = run(
        functools.partial(divide, rows, ratio),
        [((chips, rows, dim), F32), (by_cent, F32)],
        over(DP, copies),
        scale,
    )
    halves = lax.all_gather(over("z", copies), "core")
    new_centroids, masses = run(
        finish,
        [((chips, cores, rows, dim), F32), (by_cent, F32)],
        halves,
        masses,
        scratch=[pltpu.SemaphoreType.DMA((cores + 1,))],
        out_place=pltpu.HBM,
    )
    return (new_centroids.reshape(cent_local, dim), masses.reshape(cent_local))


def solution(mesh):
    dp, cent = mesh.devices.shape
    along_y = max(1, cent // 4)
    shape = (dp // 2, 2, cent // (2 * along_y), 2, along_y)
    split = Mesh(mesh.devices.reshape(shape), DP + CENT)
    return jax.shard_map(
        shards,
        mesh=split,
        in_specs=(P(DP, None), P(CENT, None), P()),
        out_specs=(P(CENT, None), P(CENT)),
        check_vma=False,
    )
```

```python
import functools
import math

import jax
import jax.numpy as jnp
from jax import lax
from jax.experimental import pallas as pl
from jax.experimental.pallas import tpu as pltpu
from jax.sharding import Mesh
from jax.sharding import PartitionSpec as P

LANES = 128
TILE = 256
DP = ("core", "z")
F32 = jnp.float32
BF16 = jnp.bfloat16


def along_lanes(a, b):
    return lax.dot_general(a, b, (((1,), (1,)), ((), ())), preferred_element_type=F32)


def plain(a, b):
    return lax.dot_general(a, b, (((1,), (0,)), ((), ())), preferred_element_type=F32)


def combine_lse(parts_ref):
    parts = parts_ref[...]
    top = jnp.max(parts, axis=0)
    return top + jnp.log(jnp.sum(jnp.exp(parts - top[None]), axis=0))


def pair_of_rows(dense, k):
    return jnp.concatenate([dense[2 * k : 2 * k + 1], dense[2 * k + 1 : 2 * k + 2]], axis=1)


def two_terms(vector):
    wide = jnp.broadcast_to(vector, (16, vector.shape[1]))
    high = wide.astype(BF16)
    low = wide - high.astype(F32)
    row = lax.broadcasted_iota(jnp.int32, wide.shape, 0)
    return jnp.where(row == 0, high.astype(F32), jnp.where(row == 1, low, 0.0)).astype(BF16)


def dense_rows(vector):
    count = vector.shape[1] // LANES
    return jnp.concatenate(
        [vector[:, k * LANES : (k + 1) * LANES] for k in range(count)], axis=0
    )


def column_sums(kept_ref, weight):
    total = None
    for k in range(kept_ref.shape[1] // TILE):
        term = along_lanes(
            two_terms(pair_of_rows(weight, k)), kept_ref[:, k * TILE : (k + 1) * TILE]
        )
        total = term if total is None else total + term
    return dense_rows(jnp.sum(total, axis=0, keepdims=True))


def row_sums(kept_ref, scale):
    total = None
    for k in range(kept_ref.shape[0] // TILE):
        term = plain(two_terms(pair_of_rows(scale, k)), kept_ref[k * TILE : (k + 1) * TILE, :])
        total = term if total is None else total + term
    return dense_rows(jnp.sum(total, axis=0, keepdims=True))


def spread_out(out_ref, dense):
    out_ref[...] = jnp.broadcast_to(dense[None], out_ref.shape)


def half_scaled(cent_ref, diag):
    scaled = (cent_ref[...].astype(F32) * diag).astype(BF16)
    return (0.5 * scaled.astype(F32)).astype(BF16)


def first_columns(tok_hbm, cent_hbm, diag_hbm, out_ref, began_ref, tok_ref, cent_ref, diag_ref, sems):
    loads = [
        pltpu.make_async_copy(cent_hbm, cent_ref, sems.at[0]),
        pltpu.make_async_copy(diag_hbm, diag_ref, sems.at[1]),
        pltpu.make_async_copy(tok_hbm, tok_ref, sems.at[2]),
    ]
    for load in loads:
        load.start()
    for load in loads:
        load.wait()
    diag = diag_ref[...]
    half = half_scaled(cent_ref, diag)
    top = total = None
    for k in range(tok_ref.shape[0] // TILE):
        tok = tok_ref[k * TILE : (k + 1) * TILE, :]
        wide = tok.astype(F32)
        norm = 0.25 * jnp.sum(wide * wide * diag, axis=1, keepdims=True)
        score = along_lanes(tok, half) - norm
        here = jnp.max(score, axis=0, keepdims=True)
        new = here if top is None else jnp.maximum(top, here)
        part = jnp.sum(jnp.exp(score - new), axis=0, keepdims=True)
        total = part if top is None else total * jnp.exp(top - new) + part
        top = new
    spread_out(out_ref, dense_rows(top + jnp.log(total)))
    began_ref[...] = jnp.zeros_like(began_ref)


def dense_norms(vectors_ref, diag, out_ref):
    for k in range(out_ref.shape[0]):
        wide = vectors_ref[k * LANES : (k + 1) * LANES, :].astype(F32)
        norm = 0.25 * jnp.sum(wide * wide * diag, axis=1, keepdims=True)
        out_ref[k : k + 1, :] = jnp.broadcast_to(norm, (LANES, LANES)).T[:1]


def prepare(tok_ref, cent_ref, diag_ref, after_ref, near_ref, half_ref, tok_norm_ref, cent_norm_ref):
    del after_ref
    diag = diag_ref[...]
    near_ref[...] = tok_ref[...]
    half_ref[...] = half_scaled(cent_ref, diag)
    dense_norms(tok_ref, diag, tok_norm_ref)
    dense_norms(cent_ref, diag, cent_norm_ref)


def first_rows(
    cent_count, parts_ref, tok_ref, half_ref, norm_ref, tok_norm_ref, kept_ref, top_ref, out_ref, sum_ref
):
    norm = norm_ref[...]
    col = (-math.log(cent_count) - (combine_lse(parts_ref) - norm)) - norm
    column = jnp.concatenate(
        [jnp.broadcast_to(col[k : k + 1], (LANES, LANES)).T for k in range(col.shape[0])], axis=0
    )
    column = jnp.concatenate([column] * (TILE // LANES), axis=1)
    half = half_ref[...]
    for k in range(tok_ref.shape[0] // TILE):
        score = along_lanes(half, tok_ref[k * TILE : (k + 1) * TILE, :]) + column
        top = jnp.max(score, axis=0, keepdims=True)
        kept = jnp.exp(score - top)
        kept_ref[:, k * TILE : (k + 1) * TILE] = kept.astype(BF16)
        total = top + jnp.log(jnp.sum(kept, axis=0, keepdims=True))
        for h in range(TILE // LANES):
            at = k * (TILE // LANES) + h
            top_ref[at : at + 1, :] = top[:, h * LANES : (h + 1) * LANES]
            sum_ref[at : at + 1, :] = total[:, h * LANES : (h + 1) * LANES]
    top_ref[...] = top_ref[...] - tok_norm_ref[...]
    spread_out(out_ref, sum_ref[...] - tok_norm_ref[...])


def second_columns(parts_ref, top_ref, kept_ref, out_ref, gain_ref):
    gain = jnp.exp(top_ref[...] - combine_lse(parts_ref))
    gain_ref[...] = gain
    spread_out(out_ref, column_sums(kept_ref, gain))


def later_rows(ratio, parts_ref, gain_ref, kept_ref, out_ref, *scale_ref):
    scale = ratio / jnp.sum(parts_ref[...], axis=0)
    if scale_ref:
        scale_ref[0][...] = scale
    spread_out(out_ref, gain_ref[...] * row_sums(kept_ref, scale))


def later_columns(parts_ref, gain_ref, kept_ref, out_ref):
    weight = gain_ref[...] / jnp.sum(parts_ref[...], axis=0)
    spread_out(out_ref, column_sums(kept_ref, weight))


def numerators(rows, parts_ref, gain_ref, kept_ref, tok_ref, out_ref):
    weight = gain_ref[...] / jnp.sum(parts_ref[...], axis=0)
    ones = jnp.ones((TILE, LANES), BF16)
    total = None
    for k in range(kept_ref.shape[1] // TILE):
        at = slice(k * TILE, (k + 1) * TILE)
        share = (kept_ref[:, at].astype(F32) * pair_of_rows(weight, k)).astype(BF16)
        term = plain(share, jnp.concatenate([tok_ref[at, :], ones], axis=1))
        total = term if total is None else total + term
    chunks = out_ref.shape[0]
    out_ref[:, :rows, :] = total[:, :LANES].reshape(chunks, rows, LANES)
    groups, per = total.shape[0] // LANES, LANES // rows
    mass = [total[g * LANES : (g + 1) * LANES, LANES:].T[:1] for g in range(groups)]
    for k in range(chunks):
        own = jnp.broadcast_to(mass[k // per], (8, LANES))
        if k % per:
            own = pltpu.roll(own, LANES - (k % per) * rows, 1)
        out_ref[k, rows:, :] = jnp.concatenate(mass + [own[: 8 - groups]], axis=0)


def divide(rows, ratio, parts_ref, scale_ref, out_ref, mass_ref):
    total = jnp.sum(parts_ref[...], axis=0)
    groups = mass_ref.shape[0]
    mass_ref[...] = total[rows : rows + groups] * scale_ref[...] / ratio
    own = total[rows + groups : rows + groups + 1]
    own = jnp.broadcast_to(own, (LANES, LANES)).T[:rows]
    spread_out(out_ref, total[:rows] / own)


def finish(cent_ref, mass_ref, cent_hbm, mass_hbm, sems):
    cores = cent_ref.shape[0]
    stores = [pltpu.make_async_copy(mass_ref, mass_hbm, sems.at[cores])]
    for c in range(cores):
        stores.append(pltpu.make_async_copy(cent_ref.at[c], cent_hbm.at[c], sems.at[c]))
    for store in stores:
        store.start()
    for store in stores:
        store.wait()


def run(
    kernel,
    outs,
    *operands,
    scratch=(),
    place=pltpu.VMEM,
    out_place=pltpu.VMEM,
    room=24,
    cost=0,
):
    return pl.pallas_call(
        kernel,
        out_shape=[jax.ShapeDtypeStruct(shape, kind) for shape, kind in outs],
        in_specs=[pl.BlockSpec(memory_space=place)] * len(operands),
        out_specs=[pl.BlockSpec(memory_space=out_place)] * len(outs),
        scratch_shapes=list(scratch),
        cost_estimate=pl.CostEstimate(flops=cost, bytes_accessed=cost, transcendentals=0)
        if cost
        else None,
        compiler_params=pltpu.CompilerParams(vmem_limit_bytes=room * 1024 * 1024),
    )(*operands)


def shards(tokens, centroids, diagonal_factors):
    chips, cores, cent = (lax.axis_size(axis) for axis in ("z", "core", "cent"))
    dp = chips * cores
    tok_local, dim = tokens.shape
    cent_local = centroids.shape[0]
    cent_count = cent_local * cent
    ratio = tok_local * dp / cent_count
    rows = cent_local // dp
    by_tok, by_cent = (tok_local // LANES, LANES), (cent_local // LANES, LANES)
    to_dp, to_cent = (dp,) + by_cent, (cent,) + by_tok

    def over(axis, copies):
        return lax.all_to_all(copies, axis, 0, 0)

    diag = diagonal_factors.reshape(1, dim)
    copies, began = run(
        first_columns,
        [(to_dp, F32), ((8, LANES), F32)],
        tokens,
        centroids,
        diag,
        scratch=[
            pltpu.VMEM((tok_local, dim), BF16),
            pltpu.VMEM((cent_local, dim), BF16),
            pltpu.VMEM((1, dim), F32),
            pltpu.SemaphoreType.DMA((3,)),
        ],
        place=pltpu.HBM,
        room=60,
    )
    near, half, tok_norm, cent_norm = run(
        prepare,
        [((tok_local, dim), BF16), ((cent_local, dim), BF16), (by_tok, F32), (by_cent, F32)],
        tokens,
        centroids,
        diag,
        began,
        cost=4 * (tok_local + cent_local) * dim,
    )
    kept, top, copies = run(
        functools.partial(first_rows, cent_count),
        [((cent_local, tok_local), BF16), (by_tok, F32), (to_cent, F32)],
        over(DP, copies),
        near,
        half,
        cent_norm,
        tok_norm,
        scratch=[pltpu.VMEM(by_tok, F32)],
    )
    copies, gain = run(
        second_columns,
        [(to_dp, F32), (by_tok, F32)],
        over("cent", copies),
        top,
        kept,
    )
    rows_of = functools.partial(later_rows, ratio)
    rows_outs = [(to_cent, F32), (by_cent, F32)]
    (copies,) = run(rows_of, rows_outs[:1], over(DP, copies), gain, kept)
    (copies,) = run(later_columns, [(to_dp, F32)], over("cent", copies), gain, kept)
    copies, scale = run(rows_of, rows_outs, over(DP, copies), gain, kept)

    packed = (dp, rows + 8, LANES)
    (copies,) = run(
        functools.partial(numerators, rows),
        [(packed, F32)],
        over("cent", copies),
        gain,
        kept,
        near,
    )
    copies, masses = run(
        functools.partial(divide, rows, ratio),
        [((chips, rows, dim), F32), (by_cent, F32)],
        over(DP, copies),
        scale,
    )
    halves = lax.all_gather(over("z", copies), "core")
    new_centroids, masses = run(
        finish,
        [((cores, chips, rows, dim), F32), (by_cent, F32)],
        halves,
        masses,
        scratch=[pltpu.SemaphoreType.DMA((cores + 1,))],
        out_place=pltpu.HBM,
    )
    return (new_centroids.reshape(cent_local, dim), masses.reshape(cent_local))


def solution(mesh):
    dp, cent = mesh.devices.shape
    split = Mesh(mesh.devices.reshape(dp // 2, 2, cent), ("z", "core", "cent"))
    return jax.shard_map(
        shards,
        mesh=split,
        in_specs=(P(("z", "core"), None), P("cent", None), P()),
        out_specs=(P("cent", None), P("cent")),
        check_vma=False,
    )
```

```python
import functools
import math

import jax
import jax.numpy as jnp
from jax import lax
from jax.experimental import pallas as pl
from jax.experimental.pallas import tpu as pltpu
from jax.sharding import Mesh
from jax.sharding import PartitionSpec as P

LANES = 128
TILE = 256
DP = ("core", "z")
F32 = jnp.float32
BF16 = jnp.bfloat16


def along_lanes(a, b):
    return lax.dot_general(a, b, (((1,), (1,)), ((), ())), preferred_element_type=F32)


def plain(a, b):
    return lax.dot_general(a, b, (((1,), (0,)), ((), ())), preferred_element_type=F32)


def combine_lse(parts_ref):
    parts = parts_ref[...]
    top = jnp.max(parts, axis=0)
    return top + jnp.log(jnp.sum(jnp.exp(parts - top[None]), axis=0))


def pair_of_rows(dense, k):
    return jnp.concatenate([dense[2 * k : 2 * k + 1], dense[2 * k + 1 : 2 * k + 2]], axis=1)


def two_terms(vector):
    wide = jnp.broadcast_to(vector, (16, vector.shape[1]))
    high = wide.astype(BF16)
    low = wide - high.astype(F32)
    row = lax.broadcasted_iota(jnp.int32, wide.shape, 0)
    return jnp.where(row == 0, high.astype(F32), jnp.where(row == 1, low, 0.0)).astype(BF16)


def dense_rows(vector):
    count = vector.shape[1] // LANES
    return jnp.concatenate(
        [vector[:, k * LANES : (k + 1) * LANES] for k in range(count)], axis=0
    )


def column_sums(kept_ref, weight):
    total = None
    for k in range(kept_ref.shape[1] // TILE):
        term = along_lanes(
            two_terms(pair_of_rows(weight, k)), kept_ref[:, k * TILE : (k + 1) * TILE]
        )
        total = term if total is None else total + term
    return dense_rows(jnp.sum(total, axis=0, keepdims=True))


def row_sums(kept_ref, scale):
    total = None
    for k in range(kept_ref.shape[0] // TILE):
        term = plain(two_terms(pair_of_rows(scale, k)), kept_ref[k * TILE : (k + 1) * TILE, :])
        total = term if total is None else total + term
    return dense_rows(jnp.sum(total, axis=0, keepdims=True))


def spread_out(out_ref, dense):
    out_ref[...] = jnp.broadcast_to(dense[None], out_ref.shape)


def half_scaled(cent_ref, diag):
    scaled = (cent_ref[...].astype(F32) * diag).astype(BF16)
    return (0.5 * scaled.astype(F32)).astype(BF16)


def first_columns(tok_hbm, cent_hbm, diag_hbm, out_ref, began_ref, tok_ref, cent_ref, diag_ref, sems):
    loads = [
        pltpu.make_async_copy(cent_hbm, cent_ref, sems.at[0]),
        pltpu.make_async_copy(diag_hbm, diag_ref, sems.at[1]),
        pltpu.make_async_copy(tok_hbm, tok_ref, sems.at[2]),
    ]
    for load in loads:
        load.start()
    for load in loads:
        load.wait()
    diag = diag_ref[...]
    half = half_scaled(cent_ref, diag)
    top = total = None
    for k in range(tok_ref.shape[0] // TILE):
        tok = tok_ref[k * TILE : (k + 1) * TILE, :]
        wide = tok.astype(F32)
        norm = 0.25 * jnp.sum(wide * wide * diag, axis=1, keepdims=True)
        score = along_lanes(tok, half) - norm
        here = jnp.max(score, axis=0, keepdims=True)
        new = here if top is None else jnp.maximum(top, here)
        part = jnp.sum(jnp.exp(score - new), axis=0, keepdims=True)
        total = part if top is None else total * jnp.exp(top - new) + part
        top = new
    spread_out(out_ref, dense_rows(top + jnp.log(total)))
    began_ref[...] = jnp.zeros_like(began_ref)


def dense_norms(vectors_ref, diag, out_ref):
    for k in range(out_ref.shape[0]):
        wide = vectors_ref[k * LANES : (k + 1) * LANES, :].astype(F32)
        norm = 0.25 * jnp.sum(wide * wide * diag, axis=1, keepdims=True)
        out_ref[k : k + 1, :] = jnp.broadcast_to(norm, (LANES, LANES)).T[:1]


def prepare(tok_ref, cent_ref, diag_ref, after_ref, near_ref, half_ref, tok_norm_ref, cent_norm_ref):
    del after_ref
    diag = diag_ref[...]
    near_ref[...] = tok_ref[...]
    half_ref[...] = half_scaled(cent_ref, diag)
    dense_norms(tok_ref, diag, tok_norm_ref)
    dense_norms(cent_ref, diag, cent_norm_ref)


def first_rows(
    cent_count, parts_ref, tok_ref, half_ref, norm_ref, tok_norm_ref, kept_ref, top_ref, out_ref, sum_ref
):
    norm = norm_ref[...]
    col = (-math.log(cent_count) - (combine_lse(parts_ref) - norm)) - norm
    column = jnp.concatenate(
        [jnp.broadcast_to(col[k : k + 1], (LANES, LANES)).T for k in range(col.shape[0])], axis=0
    )
    column = jnp.concatenate([column] * (TILE // LANES), axis=1)
    half = half_ref[...]
    for k in range(tok_ref.shape[0] // TILE):
        score = along_lanes(half, tok_ref[k * TILE : (k + 1) * TILE, :]) + column
        top = jnp.max(score, axis=0, keepdims=True)
        kept = jnp.exp(score - top)
        kept_ref[:, k * TILE : (k + 1) * TILE] = kept.astype(BF16)
        total = top + jnp.log(jnp.sum(kept, axis=0, keepdims=True))
        for h in range(TILE // LANES):
            at = k * (TILE // LANES) + h
            top_ref[at : at + 1, :] = top[:, h * LANES : (h + 1) * LANES]
            sum_ref[at : at + 1, :] = total[:, h * LANES : (h + 1) * LANES]
    top_ref[...] = top_ref[...] - tok_norm_ref[...]
    spread_out(out_ref, sum_ref[...] - tok_norm_ref[...])


def second_columns(parts_ref, top_ref, kept_ref, out_ref, gain_ref):
    gain = jnp.exp(top_ref[...] - combine_lse(parts_ref))
    gain_ref[...] = gain
    spread_out(out_ref, column_sums(kept_ref, gain))


def later_rows(ratio, parts_ref, gain_ref, kept_ref, out_ref, *scale_ref):
    scale = ratio / jnp.sum(parts_ref[...], axis=0)
    if scale_ref:
        scale_ref[0][...] = scale
    spread_out(out_ref, gain_ref[...] * row_sums(kept_ref, scale))


def later_columns(parts_ref, gain_ref, kept_ref, out_ref):
    weight = gain_ref[...] / jnp.sum(parts_ref[...], axis=0)
    spread_out(out_ref, column_sums(kept_ref, weight))


def numerators(rows, parts_ref, gain_ref, kept_ref, tok_ref, out_ref):
    weight = gain_ref[...] / jnp.sum(parts_ref[...], axis=0)
    ones = jnp.ones((TILE, LANES), BF16)
    total = None
    for k in range(kept_ref.shape[1] // TILE):
        at = slice(k * TILE, (k + 1) * TILE)
        share = (kept_ref[:, at].astype(F32) * pair_of_rows(weight, k)).astype(BF16)
        term = plain(share, jnp.concatenate([tok_ref[at, :], ones], axis=1))
        total = term if total is None else total + term
    chunks = out_ref.shape[0]
    out_ref[:, :rows, :] = total[:, :LANES].reshape(chunks, rows, LANES)
    groups, per = total.shape[0] // LANES, LANES // rows
    mass = [total[g * LANES : (g + 1) * LANES, LANES:].T[:1] for g in range(groups)]
    for k in range(chunks):
        own = jnp.broadcast_to(mass[k // per], (8, LANES))
        if k % per:
            own = pltpu.roll(own, LANES - (k % per) * rows, 1)
        out_ref[k, rows:, :] = jnp.concatenate(mass + [own[: 8 - groups]], axis=0)


def divide(rows, ratio, parts_ref, scale_ref, out_ref, mass_ref):
    total = jnp.sum(parts_ref[...], axis=0)
    groups = mass_ref.shape[0]
    mass_ref[...] = total[rows : rows + groups] * scale_ref[...] / ratio
    own = total[rows + groups : rows + groups + 1]
    own = jnp.broadcast_to(own, (LANES, LANES)).T[:rows]
    spread_out(out_ref, total[:rows] / own)


def finish(cent_ref, mass_ref, cent_hbm, mass_hbm, sems):
    stores = [
        pltpu.make_async_copy(cent_ref, cent_hbm, sems.at[0]),
        pltpu.make_async_copy(mass_ref, mass_hbm, sems.at[1]),
    ]
    for store in stores:
        store.start()
    for store in stores:
        store.wait()


def run(
    kernel,
    outs,
    *operands,
    scratch=(),
    place=pltpu.VMEM,
    out_place=pltpu.VMEM,
    room=24,
    cost=0,
):
    return pl.pallas_call(
        kernel,
        out_shape=[jax.ShapeDtypeStruct(shape, kind) for shape, kind in outs],
        in_specs=[pl.BlockSpec(memory_space=place)] * len(operands),
        out_specs=[pl.BlockSpec(memory_space=out_place)] * len(outs),
        scratch_shapes=list(scratch),
        cost_estimate=pl.CostEstimate(flops=cost, bytes_accessed=cost, transcendentals=0)
        if cost
        else None,
        compiler_params=pltpu.CompilerParams(vmem_limit_bytes=room * 1024 * 1024),
    )(*operands)


def shards(tokens, centroids, diagonal_factors):
    dp, cent = lax.axis_size(DP), lax.axis_size("cent")
    tok_local, dim = tokens.shape
    cent_local = centroids.shape[0]
    cent_count = cent_local * cent
    ratio = tok_local * dp / cent_count
    rows = cent_local // dp
    by_tok, by_cent = (tok_local // LANES, LANES), (cent_local // LANES, LANES)
    to_dp, to_cent = (dp,) + by_cent, (cent,) + by_tok

    def over(axis, copies):
        return lax.all_to_all(copies, axis, 0, 0)

    diag = diagonal_factors.reshape(1, dim)
    copies, began = run(
        first_columns,
        [(to_dp, F32), ((8, LANES), F32)],
        tokens,
        centroids,
        diag,
        scratch=[
            pltpu.VMEM((tok_local, dim), BF16),
            pltpu.VMEM((cent_local, dim), BF16),
            pltpu.VMEM((1, dim), F32),
            pltpu.SemaphoreType.DMA((3,)),
        ],
        place=pltpu.HBM,
        room=60,
    )
    near, half, tok_norm, cent_norm = run(
        prepare,
        [((tok_local, dim), BF16), ((cent_local, dim), BF16), (by_tok, F32), (by_cent, F32)],
        tokens,
        centroids,
        diag,
        began,
        cost=4 * (tok_local + cent_local) * dim,
    )
    kept, top, copies = run(
        functools.partial(first_rows, cent_count),
        [((cent_local, tok_local), BF16), (by_tok, F32), (to_cent, F32)],
        over(DP, copies),
        near,
        half,
        cent_norm,
        tok_norm,
        scratch=[pltpu.VMEM(by_tok, F32)],
    )
    copies, gain = run(
        second_columns,
        [(to_dp, F32), (by_tok, F32)],
        over("cent", copies),
        top,
        kept,
    )
    rows_of = functools.partial(later_rows, ratio)
    rows_outs = [(to_cent, F32), (by_cent, F32)]
    (copies,) = run(rows_of, rows_outs[:1], over(DP, copies), gain, kept)
    (copies,) = run(later_columns, [(to_dp, F32)], over("cent", copies), gain, kept)
    copies, scale = run(rows_of, rows_outs, over(DP, copies), gain, kept)

    packed = (dp, rows + 8, LANES)
    (copies,) = run(
        functools.partial(numerators, rows),
        [(packed, F32)],
        over("cent", copies),
        gain,
        kept,
        near,
    )
    copies, masses = run(
        functools.partial(divide, rows, ratio),
        [((dp, rows, dim), F32), (by_cent, F32)],
        over(DP, copies),
        scale,
    )
    new_centroids, masses = run(
        finish,
        [((dp, rows, dim), F32), (by_cent, F32)],
        over(DP, copies),
        masses,
        scratch=[pltpu.SemaphoreType.DMA((2,))],
        out_place=pltpu.HBM,
    )
    return (new_centroids.reshape(cent_local, dim), masses.reshape(cent_local))


def solution(mesh):
    dp, cent = mesh.devices.shape
    split = Mesh(mesh.devices.reshape(dp // 2, 2, cent), ("z", "core", "cent"))
    return jax.shard_map(
        shards,
        mesh=split,
        in_specs=(P(("z", "core"), None), P("cent", None), P()),
        out_specs=(P("cent", None), P("cent")),
        check_vma=False,
    )
```

```python
import functools
import math

import jax
import jax.numpy as jnp
from jax import lax
from jax.experimental import pallas as pl
from jax.experimental.pallas import tpu as pltpu
from jax.sharding import Mesh
from jax.sharding import PartitionSpec as P

LANES = 128
TILE = 256
PART = 4
DP = ("core", "z")
F32 = jnp.float32
BF16 = jnp.bfloat16


def along_lanes(a, b):
    return lax.dot_general(a, b, (((1,), (1,)), ((), ())), preferred_element_type=F32)


def plain(a, b):
    return lax.dot_general(a, b, (((1,), (0,)), ((), ())), preferred_element_type=F32)


def combine_lse(parts_ref):
    parts = parts_ref[...]
    top = jnp.max(parts, axis=0)
    return top + jnp.log(jnp.sum(jnp.exp(parts - top[None]), axis=0))


def pair_of_rows(dense, k):
    return jnp.concatenate([dense[2 * k : 2 * k + 1], dense[2 * k + 1 : 2 * k + 2]], axis=1)


def two_terms(vector):
    wide = jnp.broadcast_to(vector, (16, vector.shape[1]))
    high = wide.astype(BF16)
    low = wide - high.astype(F32)
    row = lax.broadcasted_iota(jnp.int32, wide.shape, 0)
    return jnp.where(row == 0, high.astype(F32), jnp.where(row == 1, low, 0.0)).astype(BF16)


def dense_rows(vector):
    count = vector.shape[1] // LANES
    return jnp.concatenate(
        [vector[:, k * LANES : (k + 1) * LANES] for k in range(count)], axis=0
    )


def column_sums(kept_ref, weight):
    total = None
    for k in range(kept_ref.shape[1] // TILE):
        term = along_lanes(
            two_terms(pair_of_rows(weight, k)), kept_ref[:, k * TILE : (k + 1) * TILE]
        )
        total = term if total is None else total + term
    return dense_rows(jnp.sum(total, axis=0, keepdims=True))


def row_sums(kept_ref, scale):
    total = None
    for k in range(kept_ref.shape[0] // TILE):
        term = plain(two_terms(pair_of_rows(scale, k)), kept_ref[k * TILE : (k + 1) * TILE, :])
        total = term if total is None else total + term
    return dense_rows(jnp.sum(total, axis=0, keepdims=True))


def spread_out(out_ref, dense):
    out_ref[...] = jnp.broadcast_to(dense[None], out_ref.shape)


def half_scaled(cent_ref, diag):
    scaled = (cent_ref[...].astype(F32) * diag).astype(BF16)
    return (0.5 * scaled.astype(F32)).astype(BF16)


def first_columns(tok_hbm, cent_hbm, diag_hbm, out_ref, began_ref, tok_ref, cent_ref, diag_ref, sems):
    loads = [
        pltpu.make_async_copy(cent_hbm, cent_ref, sems.at[0]),
        pltpu.make_async_copy(diag_hbm, diag_ref, sems.at[1]),
        pltpu.make_async_copy(tok_hbm, tok_ref, sems.at[2]),
    ]
    for load in loads:
        load.start()
    for load in loads:
        load.wait()
    diag = diag_ref[...]
    half = half_scaled(cent_ref, diag)
    top = total = None
    for k in range(tok_ref.shape[0] // TILE):
        tok = tok_ref[k * TILE : (k + 1) * TILE, :]
        wide = tok.astype(F32)
        norm = 0.25 * jnp.sum(wide * wide * diag, axis=1, keepdims=True)
        score = along_lanes(tok, half) - norm
        here = jnp.max(score, axis=0, keepdims=True)
        new = here if top is None else jnp.maximum(top, here)
        part = jnp.sum(jnp.exp(score - new), axis=0, keepdims=True)
        total = part if top is None else total * jnp.exp(top - new) + part
        top = new
    spread_out(out_ref, dense_rows(top + jnp.log(total)))
    began_ref[...] = jnp.zeros_like(began_ref)


def dense_norms(vectors_ref, diag, out_ref):
    for k in range(out_ref.shape[0]):
        wide = vectors_ref[k * LANES : (k + 1) * LANES, :].astype(F32)
        norm = 0.25 * jnp.sum(wide * wide * diag, axis=1, keepdims=True)
        out_ref[k : k + 1, :] = jnp.broadcast_to(norm, (LANES, LANES)).T[:1]


def prepare(tok_ref, cent_ref, diag_ref, after_ref, near_ref, half_ref, tok_norm_ref, cent_norm_ref):
    del after_ref
    diag = diag_ref[...]
    near_ref[...] = tok_ref[...]
    half_ref[...] = half_scaled(cent_ref, diag)
    dense_norms(tok_ref, diag, tok_norm_ref)
    dense_norms(cent_ref, diag, cent_norm_ref)


def first_rows(
    cent_count, parts_ref, tok_ref, half_ref, norm_ref, tok_norm_ref, kept_ref, top_ref, out_ref, sum_ref
):
    norm = norm_ref[...]
    col = (-math.log(cent_count) - (combine_lse(parts_ref) - norm)) - norm
    column = jnp.concatenate(
        [jnp.broadcast_to(col[k : k + 1], (LANES, LANES)).T for k in range(col.shape[0])], axis=0
    )
    column = jnp.concatenate([column] * (TILE // LANES), axis=1)
    half = half_ref[...]
    for k in range(tok_ref.shape[0] // TILE):
        score = along_lanes(half, tok_ref[k * TILE : (k + 1) * TILE, :]) + column
        top = jnp.max(score, axis=0, keepdims=True)
        kept = jnp.exp(score - top)
        kept_ref[:, k * TILE : (k + 1) * TILE] = kept.astype(BF16)
        total = top + jnp.log(jnp.sum(kept, axis=0, keepdims=True))
        for h in range(TILE // LANES):
            at = k * (TILE // LANES) + h
            top_ref[at : at + 1, :] = top[:, h * LANES : (h + 1) * LANES]
            sum_ref[at : at + 1, :] = total[:, h * LANES : (h + 1) * LANES]
    top_ref[...] = top_ref[...] - tok_norm_ref[...]
    spread_out(out_ref, sum_ref[...] - tok_norm_ref[...])


def second_columns(parts_ref, top_ref, kept_ref, out_ref, gain_ref):
    gain = jnp.exp(top_ref[...] - combine_lse(parts_ref))
    gain_ref[...] = gain
    spread_out(out_ref, column_sums(kept_ref, gain))


def later_rows(ratio, parts_ref, gain_ref, kept_ref, out_ref, *scale_ref):
    scale = ratio / jnp.sum(parts_ref[...], axis=0)
    if scale_ref:
        scale_ref[0][...] = scale
    spread_out(out_ref, gain_ref[...] * row_sums(kept_ref, scale))


def later_columns(parts_ref, gain_ref, kept_ref, out_ref):
    weight = gain_ref[...] / jnp.sum(parts_ref[...], axis=0)
    spread_out(out_ref, column_sums(kept_ref, weight))


def numerators(rows, parts_ref, gain_ref, kept_ref, tok_ref, out_ref):
    weight = gain_ref[...] / jnp.sum(parts_ref[...], axis=0)
    ones = jnp.ones((TILE, LANES), BF16)
    total = None
    for k in range(kept_ref.shape[1] // TILE):
        at = slice(k * TILE, (k + 1) * TILE)
        share = (kept_ref[:, at].astype(F32) * pair_of_rows(weight, k)).astype(BF16)
        term = plain(share, jnp.concatenate([tok_ref[at, :], ones], axis=1))
        total = term if total is None else total + term
    chunks, blocks = out_ref.shape[0], rows // PART
    out_ref[:, :blocks] = total[:, :LANES].reshape(chunks, blocks, PART, LANES)
    mass = [
        total[g * LANES : (g + 1) * LANES, LANES:].T[:1] for g in range(total.shape[0] // LANES)
    ]
    mass = jnp.concatenate(mass, axis=0)
    for g in range(mass.shape[0] // PART):
        out_ref[:, blocks + g] = jnp.broadcast_to(
            mass[None, g * PART : (g + 1) * PART], (chunks, PART, LANES)
        )


def divide(rows, ratio, parts_ref, scale_ref, out_ref, mass_ref, turned_ref):
    total = jnp.sum(parts_ref[...], axis=0)
    blocks = rows // PART
    mass = total[blocks:].reshape(mass_ref.shape)
    mass_ref[...] = mass * scale_ref[...] / ratio
    me, per = lax.axis_index(DP), LANES // rows
    group = jnp.broadcast_to(me // per, mass.shape)
    row = lax.broadcasted_iota(jnp.int32, mass.shape, 0)
    own = jnp.sum(jnp.where(row == group, mass, 0.0), axis=0, keepdims=True)
    turned_ref[...] = jnp.broadcast_to(own, (LANES, LANES)).T
    own = turned_ref[pl.ds(pl.multiple_of((me % per) * rows, rows), rows), :]
    spread_out(out_ref, total[:blocks].reshape(rows, LANES) / own)


def finish(cent_ref, mass_ref, cent_hbm, mass_hbm, sems):
    stores = [
        pltpu.make_async_copy(cent_ref, cent_hbm, sems.at[0]),
        pltpu.make_async_copy(mass_ref, mass_hbm, sems.at[1]),
    ]
    for store in stores:
        store.start()
    for store in stores:
        store.wait()


def run(
    kernel,
    outs,
    *operands,
    scratch=(),
    place=pltpu.VMEM,
    out_place=pltpu.VMEM,
    room=24,
    cost=0,
):
    return pl.pallas_call(
        kernel,
        out_shape=[jax.ShapeDtypeStruct(shape, kind) for shape, kind in outs],
        in_specs=[pl.BlockSpec(memory_space=place)] * len(operands),
        out_specs=[pl.BlockSpec(memory_space=out_place)] * len(outs),
        scratch_shapes=list(scratch),
        cost_estimate=pl.CostEstimate(flops=cost, bytes_accessed=cost, transcendentals=0)
        if cost
        else None,
        compiler_params=pltpu.CompilerParams(vmem_limit_bytes=room * 1024 * 1024),
    )(*operands)


def shards(tokens, centroids, diagonal_factors):
    dp, cent = lax.axis_size(DP), lax.axis_size("cent")
    tok_local, dim = tokens.shape
    cent_local = centroids.shape[0]
    cent_count = cent_local * cent
    ratio = tok_local * dp / cent_count
    rows = cent_local // dp
    by_tok, by_cent = (tok_local // LANES, LANES), (cent_local // LANES, LANES)
    to_dp, to_cent = (dp,) + by_cent, (cent,) + by_tok

    def over(axis, copies):
        return lax.all_to_all(copies, axis, 0, 0)

    diag = diagonal_factors.reshape(1, dim)
    copies, began = run(
        first_columns,
        [(to_dp, F32), ((8, LANES), F32)],
        tokens,
        centroids,
        diag,
        scratch=[
            pltpu.VMEM((tok_local, dim), BF16),
            pltpu.VMEM((cent_local, dim), BF16),
            pltpu.VMEM((1, dim), F32),
            pltpu.SemaphoreType.DMA((3,)),
        ],
        place=pltpu.HBM,
        room=60,
    )
    near, half, tok_norm, cent_norm = run(
        prepare,
        [((tok_local, dim), BF16), ((cent_local, dim), BF16), (by_tok, F32), (by_cent, F32)],
        tokens,
        centroids,
        diag,
        began,
        cost=4 * (tok_local + cent_local) * dim,
    )
    kept, top, copies = run(
        functools.partial(first_rows, cent_count),
        [((cent_local, tok_local), BF16), (by_tok, F32), (to_cent, F32)],
        over(DP, copies),
        near,
        half,
        cent_norm,
        tok_norm,
        scratch=[pltpu.VMEM(by_tok, F32)],
    )
    copies, gain = run(
        second_columns,
        [(to_dp, F32), (by_tok, F32)],
        over("cent", copies),
        top,
        kept,
    )
    rows_of = functools.partial(later_rows, ratio)
    rows_outs = [(to_cent, F32), (by_cent, F32)]
    (copies,) = run(rows_of, rows_outs[:1], over(DP, copies), gain, kept)
    (copies,) = run(later_columns, [(to_dp, F32)], over("cent", copies), gain, kept)
    copies, scale = run(rows_of, rows_outs, over(DP, copies), gain, kept)

    packed = (dp, rows // PART + by_cent[0] // PART, PART, LANES)
    (copies,) = run(
        functools.partial(numerators, rows),
        [(packed, F32)],
        over("cent", copies),
        gain,
        kept,
        near,
    )
    copies, masses = run(
        functools.partial(divide, rows, ratio),
        [((dp, rows, dim), F32), (by_cent, F32)],
        over(DP, copies),
        scale,
        scratch=[pltpu.VMEM((LANES, LANES), F32)],
    )
    new_centroids, masses = run(
        finish,
        [((dp, rows, dim), F32), (by_cent, F32)],
        over(DP, copies),
        masses,
        scratch=[pltpu.SemaphoreType.DMA((2,))],
        out_place=pltpu.HBM,
    )
    return (new_centroids.reshape(cent_local, dim), masses.reshape(cent_local))


def solution(mesh):
    dp, cent = mesh.devices.shape
    split = Mesh(mesh.devices.reshape(dp // 2, 2, cent), ("z", "core", "cent"))
    return jax.shard_map(
        shards,
        mesh=split,
        in_specs=(P(("z", "core"), None), P("cent", None), P()),
        out_specs=(P("cent", None), P("cent")),
        check_vma=False,
    )
```

```python
import functools
import math

import jax
import jax.numpy as jnp
from jax import lax
from jax.experimental import pallas as pl
from jax.experimental.pallas import tpu as pltpu
from jax.sharding import Mesh
from jax.sharding import PartitionSpec as P

LANES = 128
TILE = 256
PART = 4
STORES = 4
DP = ("core", "z")
F32 = jnp.float32
BF16 = jnp.bfloat16


def along_lanes(a, b):
    return lax.dot_general(a, b, (((1,), (1,)), ((), ())), preferred_element_type=F32)


def plain(a, b):
    return lax.dot_general(a, b, (((1,), (0,)), ((), ())), preferred_element_type=F32)


def combine_lse(parts_ref):
    parts = parts_ref[...]
    top = jnp.max(parts, axis=0)
    return top + jnp.log(jnp.sum(jnp.exp(parts - top[None]), axis=0))


def pair_of_rows(dense, k):
    return jnp.concatenate([dense[2 * k : 2 * k + 1], dense[2 * k + 1 : 2 * k + 2]], axis=1)


def two_terms(vector):
    wide = jnp.broadcast_to(vector, (16, vector.shape[1]))
    high = wide.astype(BF16)
    low = wide - high.astype(F32)
    row = lax.broadcasted_iota(jnp.int32, wide.shape, 0)
    return jnp.where(row == 0, high.astype(F32), jnp.where(row == 1, low, 0.0)).astype(BF16)


def dense_rows(vector):
    count = vector.shape[1] // LANES
    return jnp.concatenate(
        [vector[:, k * LANES : (k + 1) * LANES] for k in range(count)], axis=0
    )


def column_sums(kept_ref, weight):
    total = None
    for k in range(kept_ref.shape[1] // TILE):
        term = along_lanes(
            two_terms(pair_of_rows(weight, k)), kept_ref[:, k * TILE : (k + 1) * TILE]
        )
        total = term if total is None else total + term
    return dense_rows(jnp.sum(total, axis=0, keepdims=True))


def row_sums(kept_ref, scale):
    total = None
    for k in range(kept_ref.shape[0] // TILE):
        term = plain(two_terms(pair_of_rows(scale, k)), kept_ref[k * TILE : (k + 1) * TILE, :])
        total = term if total is None else total + term
    return dense_rows(jnp.sum(total, axis=0, keepdims=True))


def spread_out(out_ref, dense):
    out_ref[...] = jnp.broadcast_to(dense[None], out_ref.shape)


def half_scaled(cent_ref, diag):
    scaled = (cent_ref[...].astype(F32) * diag).astype(BF16)
    return (0.5 * scaled.astype(F32)).astype(BF16)


def first_columns(tok_hbm, cent_hbm, diag_hbm, out_ref, began_ref, tok_ref, cent_ref, diag_ref, sems):
    loads = [
        pltpu.make_async_copy(cent_hbm, cent_ref, sems.at[0]),
        pltpu.make_async_copy(diag_hbm, diag_ref, sems.at[1]),
        pltpu.make_async_copy(tok_hbm, tok_ref, sems.at[2]),
    ]
    for load in loads:
        load.start()
    for load in loads:
        load.wait()
    diag = diag_ref[...]
    half = half_scaled(cent_ref, diag)
    top = total = None
    for k in range(tok_ref.shape[0] // TILE):
        tok = tok_ref[k * TILE : (k + 1) * TILE, :]
        wide = tok.astype(F32)
        norm = 0.25 * jnp.sum(wide * wide * diag, axis=1, keepdims=True)
        score = along_lanes(tok, half) - norm
        here = jnp.max(score, axis=0, keepdims=True)
        new = here if top is None else jnp.maximum(top, here)
        part = jnp.sum(jnp.exp(score - new), axis=0, keepdims=True)
        total = part if top is None else total * jnp.exp(top - new) + part
        top = new
    spread_out(out_ref, dense_rows(top + jnp.log(total)))
    began_ref[...] = jnp.zeros_like(began_ref)


def dense_norms(vectors_ref, diag, out_ref):
    for k in range(out_ref.shape[0]):
        wide = vectors_ref[k * LANES : (k + 1) * LANES, :].astype(F32)
        norm = 0.25 * jnp.sum(wide * wide * diag, axis=1, keepdims=True)
        out_ref[k : k + 1, :] = jnp.broadcast_to(norm, (LANES, LANES)).T[:1]


def prepare(tok_ref, cent_ref, diag_ref, after_ref, near_ref, half_ref, tok_norm_ref, cent_norm_ref):
    del after_ref
    diag = diag_ref[...]
    near_ref[...] = tok_ref[...]
    half_ref[...] = half_scaled(cent_ref, diag)
    dense_norms(tok_ref, diag, tok_norm_ref)
    dense_norms(cent_ref, diag, cent_norm_ref)


def first_rows(
    cent_count, parts_ref, tok_ref, half_ref, norm_ref, tok_norm_ref, kept_ref, top_ref, out_ref, sum_ref
):
    norm = norm_ref[...]
    col = (-math.log(cent_count) - (combine_lse(parts_ref) - norm)) - norm
    column = jnp.concatenate(
        [jnp.broadcast_to(col[k : k + 1], (LANES, LANES)).T for k in range(col.shape[0])], axis=0
    )
    column = jnp.concatenate([column] * (TILE // LANES), axis=1)
    half = half_ref[...]
    for k in range(tok_ref.shape[0] // TILE):
        score = along_lanes(half, tok_ref[k * TILE : (k + 1) * TILE, :]) + column
        top = jnp.max(score, axis=0, keepdims=True)
        kept = jnp.exp(score - top)
        kept_ref[:, k * TILE : (k + 1) * TILE] = kept.astype(BF16)
        total = top + jnp.log(jnp.sum(kept, axis=0, keepdims=True))
        for h in range(TILE // LANES):
            at = k * (TILE // LANES) + h
            top_ref[at : at + 1, :] = top[:, h * LANES : (h + 1) * LANES]
            sum_ref[at : at + 1, :] = total[:, h * LANES : (h + 1) * LANES]
    top_ref[...] = top_ref[...] - tok_norm_ref[...]
    spread_out(out_ref, sum_ref[...] - tok_norm_ref[...])


def second_columns(parts_ref, top_ref, kept_ref, out_ref, gain_ref):
    gain = jnp.exp(top_ref[...] - combine_lse(parts_ref))
    gain_ref[...] = gain
    spread_out(out_ref, column_sums(kept_ref, gain))


def later_rows(ratio, parts_ref, gain_ref, kept_ref, out_ref, *scale_ref):
    scale = ratio / jnp.sum(parts_ref[...], axis=0)
    if scale_ref:
        scale_ref[0][...] = scale
    spread_out(out_ref, gain_ref[...] * row_sums(kept_ref, scale))


def later_columns(parts_ref, gain_ref, kept_ref, out_ref):
    weight = gain_ref[...] / jnp.sum(parts_ref[...], axis=0)
    spread_out(out_ref, column_sums(kept_ref, weight))


def numerators(rows, parts_ref, gain_ref, kept_ref, tok_ref, out_ref):
    weight = gain_ref[...] / jnp.sum(parts_ref[...], axis=0)
    ones = jnp.ones((TILE, LANES), BF16)
    total = None
    for k in range(kept_ref.shape[1] // TILE):
        at = slice(k * TILE, (k + 1) * TILE)
        share = (kept_ref[:, at].astype(F32) * pair_of_rows(weight, k)).astype(BF16)
        term = plain(share, jnp.concatenate([tok_ref[at, :], ones], axis=1))
        total = term if total is None else total + term
    chunks, blocks = out_ref.shape[0], rows // PART
    out_ref[:, :blocks] = total[:, :LANES].reshape(chunks, blocks, PART, LANES)
    mass = [
        total[g * LANES : (g + 1) * LANES, LANES:].T[:1] for g in range(total.shape[0] // LANES)
    ]
    mass = jnp.concatenate(mass, axis=0)
    for g in range(mass.shape[0] // PART):
        out_ref[:, blocks + g] = jnp.broadcast_to(
            mass[None, g * PART : (g + 1) * PART], (chunks, PART, LANES)
        )


def divide(rows, ratio, parts_ref, scale_ref, out_ref, mass_ref, turned_ref):
    total = jnp.sum(parts_ref[...], axis=0)
    blocks = rows // PART
    mass = total[blocks:].reshape(mass_ref.shape)
    mass_ref[...] = mass * scale_ref[...] / ratio
    me, per = lax.axis_index(DP), LANES // rows
    group = jnp.broadcast_to(me // per, mass.shape)
    row = lax.broadcasted_iota(jnp.int32, mass.shape, 0)
    own = jnp.sum(jnp.where(row == group, mass, 0.0), axis=0, keepdims=True)
    turned_ref[...] = jnp.broadcast_to(own, (LANES, LANES)).T
    own = turned_ref[pl.ds(pl.multiple_of((me % per) * rows, rows), rows), :]
    spread_out(out_ref, total[:blocks].reshape(rows, LANES) / own)


def finish(cent_ref, mass_ref, cent_hbm, mass_hbm, sems):
    stores = [pltpu.make_async_copy(mass_ref, mass_hbm, sems.at[STORES])]
    share = cent_ref.shape[0] // STORES
    for k in range(STORES):
        at = pl.ds(k * share, share)
        stores.append(pltpu.make_async_copy(cent_ref.at[at], cent_hbm.at[at], sems.at[k]))
    for store in stores:
        store.start()
    for store in stores:
        store.wait()


def run(
    kernel,
    outs,
    *operands,
    scratch=(),
    place=pltpu.VMEM,
    out_place=pltpu.VMEM,
    room=24,
    cost=0,
):
    return pl.pallas_call(
        kernel,
        out_shape=[jax.ShapeDtypeStruct(shape, kind) for shape, kind in outs],
        in_specs=[pl.BlockSpec(memory_space=place)] * len(operands),
        out_specs=[pl.BlockSpec(memory_space=out_place)] * len(outs),
        scratch_shapes=list(scratch),
        cost_estimate=pl.CostEstimate(flops=cost, bytes_accessed=cost, transcendentals=0)
        if cost
        else None,
        compiler_params=pltpu.CompilerParams(vmem_limit_bytes=room * 1024 * 1024),
    )(*operands)


def shards(tokens, centroids, diagonal_factors):
    dp, cent = lax.axis_size(DP), lax.axis_size("cent")
    tok_local, dim = tokens.shape
    cent_local = centroids.shape[0]
    cent_count = cent_local * cent
    ratio = tok_local * dp / cent_count
    rows = cent_local // dp
    by_tok, by_cent = (tok_local // LANES, LANES), (cent_local // LANES, LANES)
    to_dp, to_cent = (dp,) + by_cent, (cent,) + by_tok

    def over(axis, copies):
        return lax.all_to_all(copies, axis, 0, 0)

    diag = diagonal_factors.reshape(1, dim)
    copies, began = run(
        first_columns,
        [(to_dp, F32), ((8, LANES), F32)],
        tokens,
        centroids,
        diag,
        scratch=[
            pltpu.VMEM((tok_local, dim), BF16),
            pltpu.VMEM((cent_local, dim), BF16),
            pltpu.VMEM((1, dim), F32),
            pltpu.SemaphoreType.DMA((3,)),
        ],
        place=pltpu.HBM,
        room=60,
    )
    near, half, tok_norm, cent_norm = run(
        prepare,
        [((tok_local, dim), BF16), ((cent_local, dim), BF16), (by_tok, F32), (by_cent, F32)],
        tokens,
        centroids,
        diag,
        began,
        cost=4 * (tok_local + cent_local) * dim,
    )
    kept, top, copies = run(
        functools.partial(first_rows, cent_count),
        [((cent_local, tok_local), BF16), (by_tok, F32), (to_cent, F32)],
        over(DP, copies),
        near,
        half,
        cent_norm,
        tok_norm,
        scratch=[pltpu.VMEM(by_tok, F32)],
    )
    copies, gain = run(
        second_columns,
        [(to_dp, F32), (by_tok, F32)],
        over("cent", copies),
        top,
        kept,
    )
    rows_of = functools.partial(later_rows, ratio)
    rows_outs = [(to_cent, F32), (by_cent, F32)]
    (copies,) = run(rows_of, rows_outs[:1], over(DP, copies), gain, kept)
    (copies,) = run(later_columns, [(to_dp, F32)], over("cent", copies), gain, kept)
    copies, scale = run(rows_of, rows_outs, over(DP, copies), gain, kept)

    packed = (dp, rows // PART + by_cent[0] // PART, PART, LANES)
    (copies,) = run(
        functools.partial(numerators, rows),
        [(packed, F32)],
        over("cent", copies),
        gain,
        kept,
        near,
    )
    copies, masses = run(
        functools.partial(divide, rows, ratio),
        [((dp, rows, dim), F32), (by_cent, F32)],
        over(DP, copies),
        scale,
        scratch=[pltpu.VMEM((LANES, LANES), F32)],
    )
    new_centroids, masses = run(
        finish,
        [((dp, rows, dim), F32), (by_cent, F32)],
        over(DP, copies),
        masses,
        scratch=[pltpu.SemaphoreType.DMA((STORES + 1,))],
        out_place=pltpu.HBM,
    )
    return (new_centroids.reshape(cent_local, dim), masses.reshape(cent_local))


def solution(mesh):
    dp, cent = mesh.devices.shape
    split = Mesh(mesh.devices.reshape(dp // 2, 2, cent), ("z", "core", "cent"))
    return jax.shard_map(
        shards,
        mesh=split,
        in_specs=(P(("z", "core"), None), P("cent", None), P()),
        out_specs=(P("cent", None), P("cent")),
        check_vma=False,
    )
```

```python
import functools
import math

import jax
import jax.numpy as jnp
from jax import lax
from jax.experimental import pallas as pl
from jax.experimental.pallas import tpu as pltpu
from jax.sharding import Mesh
from jax.sharding import PartitionSpec as P

LANES = 128
TILE = 256
PART = 4
DP = ("core", "z")
F32 = jnp.float32
BF16 = jnp.bfloat16


def along_lanes(a, b):
    return lax.dot_general(a, b, (((1,), (1,)), ((), ())), preferred_element_type=F32)


def plain(a, b):
    return lax.dot_general(a, b, (((1,), (0,)), ((), ())), preferred_element_type=F32)


def combine_lse(parts_ref):
    parts = parts_ref[...]
    top = jnp.max(parts, axis=0)
    return top + jnp.log(jnp.sum(jnp.exp(parts - top[None]), axis=0))


def pair_of_rows(dense, k):
    return jnp.concatenate([dense[2 * k : 2 * k + 1], dense[2 * k + 1 : 2 * k + 2]], axis=1)


def two_terms(vector):
    wide = jnp.broadcast_to(vector, (16, vector.shape[1]))
    high = wide.astype(BF16)
    low = wide - high.astype(F32)
    row = lax.broadcasted_iota(jnp.int32, wide.shape, 0)
    return jnp.where(row == 0, high.astype(F32), jnp.where(row == 1, low, 0.0)).astype(BF16)


def dense_rows(vector):
    count = vector.shape[1] // LANES
    return jnp.concatenate(
        [vector[:, k * LANES : (k + 1) * LANES] for k in range(count)], axis=0
    )


def column_sums(kept_ref, weight):
    total = None
    for k in range(kept_ref.shape[1] // TILE):
        term = along_lanes(
            two_terms(pair_of_rows(weight, k)), kept_ref[:, k * TILE : (k + 1) * TILE]
        )
        total = term if total is None else total + term
    return dense_rows(jnp.sum(total, axis=0, keepdims=True))


def row_sums(kept_ref, scale):
    total = None
    for k in range(kept_ref.shape[0] // TILE):
        term = plain(two_terms(pair_of_rows(scale, k)), kept_ref[k * TILE : (k + 1) * TILE, :])
        total = term if total is None else total + term
    return dense_rows(jnp.sum(total, axis=0, keepdims=True))


def spread_out(out_ref, dense):
    out_ref[...] = jnp.broadcast_to(dense[None], out_ref.shape)


def half_scaled(cent_ref, diag):
    scaled = (cent_ref[...].astype(F32) * diag).astype(BF16)
    return (0.5 * scaled.astype(F32)).astype(BF16)


def first_columns(tok_hbm, cent_hbm, diag_hbm, out_ref, began_ref, tok_ref, cent_ref, diag_ref, sems):
    loads = [
        pltpu.make_async_copy(cent_hbm, cent_ref, sems.at[0]),
        pltpu.make_async_copy(diag_hbm, diag_ref, sems.at[1]),
        pltpu.make_async_copy(tok_hbm, tok_ref, sems.at[2]),
    ]
    for load in loads:
        load.start()
    for load in loads:
        load.wait()
    diag = diag_ref[...]
    half = half_scaled(cent_ref, diag)
    top = total = None
    for k in range(tok_ref.shape[0] // TILE):
        tok = tok_ref[k * TILE : (k + 1) * TILE, :]
        wide = tok.astype(F32)
        norm = 0.25 * jnp.sum(wide * wide * diag, axis=1, keepdims=True)
        score = along_lanes(tok, half) - norm
        here = jnp.max(score, axis=0, keepdims=True)
        new = here if top is None else jnp.maximum(top, here)
        part = jnp.sum(jnp.exp(score - new), axis=0, keepdims=True)
        total = part if top is None else total * jnp.exp(top - new) + part
        top = new
    spread_out(out_ref, dense_rows(top + jnp.log(total)))
    began_ref[...] = jnp.zeros_like(began_ref)


def dense_norms(vectors_ref, diag, out_ref):
    for k in range(out_ref.shape[0]):
        wide = vectors_ref[k * LANES : (k + 1) * LANES, :].astype(F32)
        norm = 0.25 * jnp.sum(wide * wide * diag, axis=1, keepdims=True)
        out_ref[k : k + 1, :] = jnp.broadcast_to(norm, (LANES, LANES)).T[:1]


def prepare(tok_ref, cent_ref, diag_ref, after_ref, near_ref, half_ref, tok_norm_ref, cent_norm_ref):
    del after_ref
    diag = diag_ref[...]
    near_ref[...] = tok_ref[...]
    half_ref[...] = half_scaled(cent_ref, diag)
    dense_norms(tok_ref, diag, tok_norm_ref)
    dense_norms(cent_ref, diag, cent_norm_ref)


def first_rows(
    cent_count, parts_ref, tok_ref, half_ref, norm_ref, tok_norm_ref, kept_ref, top_ref, out_ref, sum_ref
):
    norm = norm_ref[...]
    col = (-math.log(cent_count) - (combine_lse(parts_ref) - norm)) - norm
    column = jnp.concatenate(
        [jnp.broadcast_to(col[k : k + 1], (LANES, LANES)).T for k in range(col.shape[0])], axis=0
    )
    column = jnp.concatenate([column] * (TILE // LANES), axis=1)
    half = half_ref[...]
    for k in range(tok_ref.shape[0] // TILE):
        score = along_lanes(half, tok_ref[k * TILE : (k + 1) * TILE, :]) + column
        top = jnp.max(score, axis=0, keepdims=True)
        kept = jnp.exp(score - top)
        kept_ref[:, k * TILE : (k + 1) * TILE] = kept.astype(BF16)
        total = top + jnp.log(jnp.sum(kept, axis=0, keepdims=True))
        for h in range(TILE // LANES):
            at = k * (TILE // LANES) + h
            top_ref[at : at + 1, :] = top[:, h * LANES : (h + 1) * LANES]
            sum_ref[at : at + 1, :] = total[:, h * LANES : (h + 1) * LANES]
    top_ref[...] = top_ref[...] - tok_norm_ref[...]
    spread_out(out_ref, sum_ref[...] - tok_norm_ref[...])


def second_columns(parts_ref, top_ref, kept_ref, out_ref, gain_ref):
    gain = jnp.exp(top_ref[...] - combine_lse(parts_ref))
    gain_ref[...] = gain
    spread_out(out_ref, column_sums(kept_ref, gain))


def later_rows(ratio, parts_ref, gain_ref, kept_ref, out_ref, *scale_ref):
    scale = ratio / jnp.sum(parts_ref[...], axis=0)
    if scale_ref:
        scale_ref[0][...] = scale
    spread_out(out_ref, gain_ref[...] * row_sums(kept_ref, scale))


def later_columns(parts_ref, gain_ref, kept_ref, out_ref):
    weight = gain_ref[...] / jnp.sum(parts_ref[...], axis=0)
    spread_out(out_ref, column_sums(kept_ref, weight))


def numerators(rows, parts_ref, gain_ref, kept_ref, tok_ref, out_ref):
    weight = gain_ref[...] / jnp.sum(parts_ref[...], axis=0)
    ones = jnp.ones((TILE, LANES), BF16)
    total = None
    for k in range(kept_ref.shape[1] // TILE):
        at = slice(k * TILE, (k + 1) * TILE)
        share = (kept_ref[:, at].astype(F32) * pair_of_rows(weight, k)).astype(BF16)
        term = plain(share, jnp.concatenate([tok_ref[at, :], ones], axis=1))
        total = term if total is None else total + term
    chunks, blocks = out_ref.shape[0], rows // PART
    out_ref[:, :blocks] = total[:, :LANES].reshape(chunks, blocks, PART, LANES)
    mass = [
        total[g * LANES : (g + 1) * LANES, LANES:].T[:1] for g in range(total.shape[0] // LANES)
    ]
    mass = jnp.concatenate(mass, axis=0)
    for g in range(mass.shape[0] // PART):
        out_ref[:, blocks + g] = jnp.broadcast_to(
            mass[None, g * PART : (g + 1) * PART], (chunks, PART, LANES)
        )


def divide(rows, ratio, parts_ref, scale_ref, out_ref, mass_ref, turned_ref):
    total = jnp.sum(parts_ref[...], axis=0)
    blocks = rows // PART
    mass = total[blocks:].reshape(mass_ref.shape)
    mass_ref[...] = mass * scale_ref[...] / ratio
    me, per = lax.axis_index(DP), LANES // rows
    group = jnp.broadcast_to(me // per, mass.shape)
    row = lax.broadcasted_iota(jnp.int32, mass.shape, 0)
    own = jnp.sum(jnp.where(row == group, mass, 0.0), axis=0, keepdims=True)
    turned_ref[...] = jnp.broadcast_to(own, (LANES, LANES)).T
    own = turned_ref[pl.ds(pl.multiple_of((me % per) * rows, rows), rows), :]
    spread_out(out_ref, (total[:blocks].reshape(rows, LANES) / own).reshape(blocks, PART, LANES))


def finish(cent_ref, mass_ref, cent_hbm, mass_hbm, sems):
    stores = [
        pltpu.make_async_copy(cent_ref, cent_hbm, sems.at[0]),
        pltpu.make_async_copy(mass_ref, mass_hbm, sems.at[1]),
    ]
    for store in stores:
        store.start()
    for store in stores:
        store.wait()


def run(
    kernel,
    outs,
    *operands,
    scratch=(),
    place=pltpu.VMEM,
    out_place=pltpu.VMEM,
    room=24,
    cost=0,
):
    return pl.pallas_call(
        kernel,
        out_shape=[jax.ShapeDtypeStruct(shape, kind) for shape, kind in outs],
        in_specs=[pl.BlockSpec(memory_space=place)] * len(operands),
        out_specs=[pl.BlockSpec(memory_space=out_place)] * len(outs),
        scratch_shapes=list(scratch),
        cost_estimate=pl.CostEstimate(flops=cost, bytes_accessed=cost, transcendentals=0)
        if cost
        else None,
        compiler_params=pltpu.CompilerParams(vmem_limit_bytes=room * 1024 * 1024),
    )(*operands)


def shards(tokens, centroids, diagonal_factors):
    dp, cent = lax.axis_size(DP), lax.axis_size("cent")
    tok_local, dim = tokens.shape
    cent_local = centroids.shape[0]
    cent_count = cent_local * cent
    ratio = tok_local * dp / cent_count
    rows = cent_local // dp
    by_tok, by_cent = (tok_local // LANES, LANES), (cent_local // LANES, LANES)
    to_dp, to_cent = (dp,) + by_cent, (cent,) + by_tok

    def over(axis, copies):
        return lax.all_to_all(copies, axis, 0, 0)

    diag = diagonal_factors.reshape(1, dim)
    copies, began = run(
        first_columns,
        [(to_dp, F32), ((8, LANES), F32)],
        tokens,
        centroids,
        diag,
        scratch=[
            pltpu.VMEM((tok_local, dim), BF16),
            pltpu.VMEM((cent_local, dim), BF16),
            pltpu.VMEM((1, dim), F32),
            pltpu.SemaphoreType.DMA((3,)),
        ],
        place=pltpu.HBM,
        room=60,
    )
    near, half, tok_norm, cent_norm = run(
        prepare,
        [((tok_local, dim), BF16), ((cent_local, dim), BF16), (by_tok, F32), (by_cent, F32)],
        tokens,
        centroids,
        diag,
        began,
        cost=4 * (tok_local + cent_local) * dim,
    )
    kept, top, copies = run(
        functools.partial(first_rows, cent_count),
        [((cent_local, tok_local), BF16), (by_tok, F32), (to_cent, F32)],
        over(DP, copies),
        near,
        half,
        cent_norm,
        tok_norm,
        scratch=[pltpu.VMEM(by_tok, F32)],
    )
    copies, gain = run(
        second_columns,
        [(to_dp, F32), (by_tok, F32)],
        over("cent", copies),
        top,
        kept,
    )
    rows_of = functools.partial(later_rows, ratio)
    rows_outs = [(to_cent, F32), (by_cent, F32)]
    (copies,) = run(rows_of, rows_outs[:1], over(DP, copies), gain, kept)
    (copies,) = run(later_columns, [(to_dp, F32)], over("cent", copies), gain, kept)
    copies, scale = run(rows_of, rows_outs, over(DP, copies), gain, kept)

    packed = (dp, rows // PART + by_cent[0] // PART, PART, LANES)
    (copies,) = run(
        functools.partial(numerators, rows),
        [(packed, F32)],
        over("cent", copies),
        gain,
        kept,
        near,
    )
    copies, masses = run(
        functools.partial(divide, rows, ratio),
        [((dp, rows // PART, PART, dim), F32), (by_cent, F32)],
        over(DP, copies),
        scale,
        scratch=[pltpu.VMEM((LANES, LANES), F32)],
    )
    new_centroids, masses = run(
        finish,
        [((dp, rows // PART, PART, dim), F32), (by_cent, F32)],
        over(DP, copies),
        masses,
        scratch=[pltpu.SemaphoreType.DMA((2,))],
        out_place=pltpu.HBM,
    )
    return (new_centroids.reshape(cent_local, dim), masses.reshape(cent_local))


def solution(mesh):
    dp, cent = mesh.devices.shape
    split = Mesh(mesh.devices.reshape(dp // 2, 2, cent), ("z", "core", "cent"))
    return jax.shard_map(
        shards,
        mesh=split,
        in_specs=(P(("z", "core"), None), P("cent", None), P()),
        out_specs=(P("cent", None), P("cent")),
        check_vma=False,
    )
```

```python
import functools
import math

import jax
import jax.numpy as jnp
from jax import lax
from jax.experimental import pallas as pl
from jax.experimental.pallas import tpu as pltpu
from jax.sharding import Mesh
from jax.sharding import PartitionSpec as P

LANES = 128
TILE = 256
PART = 4
DP = ("core", "z")
CENT = ("y", "x")
F32 = jnp.float32
BF16 = jnp.bfloat16


def along_lanes(a, b):
    return lax.dot_general(a, b, (((1,), (1,)), ((), ())), preferred_element_type=F32)


def plain(a, b):
    return lax.dot_general(a, b, (((1,), (0,)), ((), ())), preferred_element_type=F32)


def combine_lse(parts_ref):
    parts = parts_ref[...]
    top = jnp.max(parts, axis=0)
    return top + jnp.log(jnp.sum(jnp.exp(parts - top[None]), axis=0))


def pair_of_rows(dense, k):
    return jnp.concatenate([dense[2 * k : 2 * k + 1], dense[2 * k + 1 : 2 * k + 2]], axis=1)


def two_terms(vector):
    wide = jnp.broadcast_to(vector, (16, vector.shape[1]))
    high = wide.astype(BF16)
    low = wide - high.astype(F32)
    row = lax.broadcasted_iota(jnp.int32, wide.shape, 0)
    return jnp.where(row == 0, high.astype(F32), jnp.where(row == 1, low, 0.0)).astype(BF16)


def dense_rows(vector):
    count = vector.shape[1] // LANES
    return jnp.concatenate(
        [vector[:, k * LANES : (k + 1) * LANES] for k in range(count)], axis=0
    )


def column_sums(kept_ref, weight):
    total = None
    for k in range(kept_ref.shape[1] // TILE):
        term = along_lanes(
            two_terms(pair_of_rows(weight, k)), kept_ref[:, k * TILE : (k + 1) * TILE]
        )
        total = term if total is None else total + term
    return dense_rows(jnp.sum(total, axis=0, keepdims=True))


def row_sums(kept_ref, scale):
    total = None
    for k in range(kept_ref.shape[0] // TILE):
        term = plain(two_terms(pair_of_rows(scale, k)), kept_ref[k * TILE : (k + 1) * TILE, :])
        total = term if total is None else total + term
    return dense_rows(jnp.sum(total, axis=0, keepdims=True))


def spread_out(out_ref, dense):
    out_ref[...] = jnp.broadcast_to(dense[None], out_ref.shape)


def half_scaled(cent_ref, diag):
    scaled = (cent_ref[...].astype(F32) * diag).astype(BF16)
    return (0.5 * scaled.astype(F32)).astype(BF16)


def first_columns(tok_hbm, cent_hbm, diag_hbm, out_ref, began_ref, tok_ref, cent_ref, diag_ref, sems):
    loads = [
        pltpu.make_async_copy(cent_hbm, cent_ref, sems.at[0]),
        pltpu.make_async_copy(diag_hbm, diag_ref, sems.at[1]),
        pltpu.make_async_copy(tok_hbm, tok_ref, sems.at[2]),
    ]
    for load in loads:
        load.start()
    for load in loads:
        load.wait()
    diag = diag_ref[...]
    half = half_scaled(cent_ref, diag)
    top = total = None
    for k in range(tok_ref.shape[0] // TILE):
        tok = tok_ref[k * TILE : (k + 1) * TILE, :]
        wide = tok.astype(F32)
        norm = 0.25 * jnp.sum(wide * wide * diag, axis=1, keepdims=True)
        score = along_lanes(tok, half) - norm
        here = jnp.max(score, axis=0, keepdims=True)
        new = here if top is None else jnp.maximum(top, here)
        part = jnp.sum(jnp.exp(score - new), axis=0, keepdims=True)
        total = part if top is None else total * jnp.exp(top - new) + part
        top = new
    spread_out(out_ref, dense_rows(top + jnp.log(total)))
    began_ref[...] = jnp.zeros_like(began_ref)


def dense_norms(vectors_ref, diag, out_ref):
    for k in range(out_ref.shape[0]):
        wide = vectors_ref[k * LANES : (k + 1) * LANES, :].astype(F32)
        norm = 0.25 * jnp.sum(wide * wide * diag, axis=1, keepdims=True)
        out_ref[k : k + 1, :] = jnp.broadcast_to(norm, (LANES, LANES)).T[:1]


def prepare(tok_ref, cent_ref, diag_ref, after_ref, near_ref, half_ref, tok_norm_ref, cent_norm_ref):
    del after_ref
    diag = diag_ref[...]
    near_ref[...] = tok_ref[...]
    half_ref[...] = half_scaled(cent_ref, diag)
    dense_norms(tok_ref, diag, tok_norm_ref)
    dense_norms(cent_ref, diag, cent_norm_ref)


def first_rows(
    cent_count, parts_ref, tok_ref, half_ref, norm_ref, tok_norm_ref, kept_ref, top_ref, out_ref, sum_ref
):
    norm = norm_ref[...]
    col = (-math.log(cent_count) - (combine_lse(parts_ref) - norm)) - norm
    column = jnp.concatenate(
        [jnp.broadcast_to(col[k : k + 1], (LANES, LANES)).T for k in range(col.shape[0])], axis=0
    )
    column = jnp.concatenate([column] * (TILE // LANES), axis=1)
    half = half_ref[...]
    for k in range(tok_ref.shape[0] // TILE):
        score = along_lanes(half, tok_ref[k * TILE : (k + 1) * TILE, :]) + column
        top = jnp.max(score, axis=0, keepdims=True)
        kept = jnp.exp(score - top)
        kept_ref[:, k * TILE : (k + 1) * TILE] = kept.astype(BF16)
        total = top + jnp.log(jnp.sum(kept, axis=0, keepdims=True))
        for h in range(TILE // LANES):
            at = k * (TILE // LANES) + h
            top_ref[at : at + 1, :] = top[:, h * LANES : (h + 1) * LANES]
            sum_ref[at : at + 1, :] = total[:, h * LANES : (h + 1) * LANES]
    top_ref[...] = top_ref[...] - tok_norm_ref[...]
    spread_out(out_ref, sum_ref[...] - tok_norm_ref[...])


def second_columns(parts_ref, top_ref, kept_ref, out_ref, gain_ref):
    gain = jnp.exp(top_ref[...] - combine_lse(parts_ref))
    gain_ref[...] = gain
    spread_out(out_ref, column_sums(kept_ref, gain))


def later_rows(ratio, parts_ref, gain_ref, kept_ref, out_ref, *scale_ref):
    scale = ratio / jnp.sum(parts_ref[...], axis=0)
    if scale_ref:
        scale_ref[0][...] = scale
    spread_out(out_ref, gain_ref[...] * row_sums(kept_ref, scale))


def later_columns(parts_ref, gain_ref, kept_ref, out_ref):
    weight = gain_ref[...] / jnp.sum(parts_ref[...], axis=0)
    spread_out(out_ref, column_sums(kept_ref, weight))


def numerators(rows, parts_ref, gain_ref, kept_ref, tok_ref, out_ref):
    weight = gain_ref[...] / jnp.sum(parts_ref[...], axis=0)
    ones = jnp.ones((TILE, LANES), BF16)
    total = None
    for k in range(kept_ref.shape[1] // TILE):
        at = slice(k * TILE, (k + 1) * TILE)
        share = (kept_ref[:, at].astype(F32) * pair_of_rows(weight, k)).astype(BF16)
        term = plain(share, jnp.concatenate([tok_ref[at, :], ones], axis=1))
        total = term if total is None else total + term
    chunks, blocks = out_ref.shape[0], rows // PART
    out_ref[:, :blocks] = total[:, :LANES].reshape(chunks, blocks, PART, LANES)
    mass = [
        total[g * LANES : (g + 1) * LANES, LANES:].T[:1] for g in range(total.shape[0] // LANES)
    ]
    mass = jnp.concatenate(mass, axis=0)
    for g in range(mass.shape[0] // PART):
        out_ref[:, blocks + g] = jnp.broadcast_to(
            mass[None, g * PART : (g + 1) * PART], (chunks, PART, LANES)
        )


def divide(rows, ratio, parts_ref, scale_ref, out_ref, mass_ref, turned_ref):
    total = jnp.sum(parts_ref[...], axis=0)
    blocks = rows // PART
    mass = total[blocks:].reshape(mass_ref.shape)
    mass_ref[...] = mass * scale_ref[...] / ratio
    me, per = lax.axis_index(DP), LANES // rows
    group = jnp.broadcast_to(me // per, mass.shape)
    row = lax.broadcasted_iota(jnp.int32, mass.shape, 0)
    own = jnp.sum(jnp.where(row == group, mass, 0.0), axis=0, keepdims=True)
    turned_ref[...] = jnp.broadcast_to(own, (LANES, LANES)).T
    own = turned_ref[pl.ds(pl.multiple_of((me % per) * rows, rows), rows), :]
    spread_out(out_ref, total[:blocks].reshape(rows, LANES) / own)


def finish(cent_ref, mass_ref, cent_hbm, mass_hbm, sems):
    stores = [
        pltpu.make_async_copy(cent_ref, cent_hbm, sems.at[0]),
        pltpu.make_async_copy(mass_ref, mass_hbm, sems.at[1]),
    ]
    for store in stores:
        store.start()
    for store in stores:
        store.wait()


def run(
    kernel,
    outs,
    *operands,
    scratch=(),
    place=pltpu.VMEM,
    out_place=pltpu.VMEM,
    room=24,
    cost=0,
):
    return pl.pallas_call(
        kernel,
        out_shape=[jax.ShapeDtypeStruct(shape, kind) for shape, kind in outs],
        in_specs=[pl.BlockSpec(memory_space=place)] * len(operands),
        out_specs=[pl.BlockSpec(memory_space=out_place)] * len(outs),
        scratch_shapes=list(scratch),
        cost_estimate=pl.CostEstimate(flops=cost, bytes_accessed=cost, transcendentals=0)
        if cost
        else None,
        compiler_params=pltpu.CompilerParams(vmem_limit_bytes=room * 1024 * 1024),
    )(*operands)


def shards(tokens, centroids, diagonal_factors):
    dp, cent = lax.axis_size(DP), lax.axis_size(CENT)
    tok_local, dim = tokens.shape
    cent_local = centroids.shape[0]
    cent_count = cent_local * cent
    ratio = tok_local * dp / cent_count
    rows = cent_local // dp
    by_tok, by_cent = (tok_local // LANES, LANES), (cent_local // LANES, LANES)
    to_dp, to_cent = (dp,) + by_cent, (cent,) + by_tok

    def over(axis, copies):
        return lax.all_to_all(copies, axis, 0, 0)

    diag = diagonal_factors.reshape(1, dim)
    copies, began = run(
        first_columns,
        [(to_dp, F32), ((8, LANES), F32)],
        tokens,
        centroids,
        diag,
        scratch=[
            pltpu.VMEM((tok_local, dim), BF16),
            pltpu.VMEM((cent_local, dim), BF16),
            pltpu.VMEM((1, dim), F32),
            pltpu.SemaphoreType.DMA((3,)),
        ],
        place=pltpu.HBM,
        room=60,
    )
    near, half, tok_norm, cent_norm = run(
        prepare,
        [((tok_local, dim), BF16), ((cent_local, dim), BF16), (by_tok, F32), (by_cent, F32)],
        tokens,
        centroids,
        diag,
        began,
        cost=4 * (tok_local + cent_local) * dim,
    )
    kept, top, copies = run(
        functools.partial(first_rows, cent_count),
        [((cent_local, tok_local), BF16), (by_tok, F32), (to_cent, F32)],
        over(DP, copies),
        near,
        half,
        cent_norm,
        tok_norm,
        scratch=[pltpu.VMEM(by_tok, F32)],
    )
    copies, gain = run(
        second_columns,
        [(to_dp, F32), (by_tok, F32)],
        over(CENT, copies),
        top,
        kept,
    )
    rows_of = functools.partial(later_rows, ratio)
    rows_outs = [(to_cent, F32), (by_cent, F32)]
    (copies,) = run(rows_of, rows_outs[:1], over(DP, copies), gain, kept)
    (copies,) = run(later_columns, [(to_dp, F32)], over(CENT, copies), gain, kept)
    copies, scale = run(rows_of, rows_outs, over(DP, copies), gain, kept)

    packed = (dp, rows // PART + by_cent[0] // PART, PART, LANES)
    (copies,) = run(
        functools.partial(numerators, rows),
        [(packed, F32)],
        over(CENT, copies),
        gain,
        kept,
        near,
    )
    copies, masses = run(
        functools.partial(divide, rows, ratio),
        [((dp, rows, dim), F32), (by_cent, F32)],
        over(DP, copies),
        scale,
        scratch=[pltpu.VMEM((LANES, LANES), F32)],
    )
    new_centroids, masses = run(
        finish,
        [((dp, rows, dim), F32), (by_cent, F32)],
        over(DP, copies),
        masses,
        scratch=[pltpu.SemaphoreType.DMA((2,))],
        out_place=pltpu.HBM,
    )
    return (new_centroids.reshape(cent_local, dim), masses.reshape(cent_local))


def solution(mesh):
    dp, cent = mesh.devices.shape
    split = Mesh(mesh.devices.reshape(dp // 2, 2, 4, cent // 4), ("z", "core", "x", "y"))
    return jax.shard_map(
        shards,
        mesh=split,
        in_specs=(P(("z", "core"), None), P(("x", "y"), None), P()),
        out_specs=(P(("x", "y"), None), P(("x", "y"))),
        check_vma=False,
    )
```
